32 devices in a mesh: rows: 32 (over z, y, x, core), users: 1.
Axes of the slice: x: 2, y: 2, z: 4, core: 2. Of those that a mesh axis runs over, the one named last changes fastest.
Arguments:
- old_basis: bfloat16 [12288, 4096], P('rows', 'users'), may hold values from -24 to 24
- new_atoms: bfloat16 [12288, 128], P('rows'), may hold values from -300 to 300
- user_residuals: bfloat16 [12288, 128], P('rows', 'users'), may hold values from -850 to 850
Outputs:
- new_block: bfloat16 [12288, 128], P('rows')
- updated_residuals: bfloat16 [12288, 128], P('rows', 'users')
The draws below stay inside these ranges and needn't reach their ends.
All inputs are finite; a program needn't handle non-finite values.
Results may differ from the reference program's by a relative error of at most 0.019.
Values may be sent and summed in bfloat16 or wider, within the bound.
No kernel may reach another device: no remote copies, remote signals or barrier semaphores. Data moves between devices by JAX's collectives and lax.ppermute only.
A program may use at most 64 MiB of HBM per device.

```python
import math
import jax
import jax.numpy as jnp
from jax import lax

M_DEV = 384
K = 4096
B = 128
M = 12288
U = 128
N_ROWS = 32


def spread_pair(blocks, share):
    high = math.sqrt(blocks * share)
    rest = math.sqrt(blocks * (1.0 - share) / max(blocks - 1, 1))
    return (high, rest)


def basis_column(key, column):
    blocks = M // M_DEV
    high, rest = spread_pair(blocks, 0.25)
    owners = jax.random.permutation(jax.random.fold_in(key, 12), blocks)
    target = owners[column % blocks]
    column_key = jax.random.fold_in(jax.random.fold_in(key, 11), column)
    noise = jax.random.truncated_normal(column_key, -4.0, 4.0, (M,), jnp.float32)
    owner_row = jnp.arange(M, dtype=jnp.int32) // M_DEV
    return noise * jnp.where(owner_row == target, high, rest)


def fresh_atoms(key):
    blocks = M // M_DEV
    high, rest = spread_pair(blocks, 1.0 / 3.0)
    base_noise = jax.random.truncated_normal(jax.random.fold_in(key, 21), -4.0, 4.0, (M, B), jnp.float32)
    row_scale = jnp.exp(jax.random.uniform(jax.random.fold_in(key, 23), (M, 1), jnp.float32, 0.0, math.log(10.0)))
    mixed = base_noise + 0.5 * jnp.roll(base_noise, -1, axis=1) - 0.4 * jnp.roll(base_noise, -7, axis=1)
    col_scale = jnp.exp(jax.random.uniform(jax.random.fold_in(key, 24), (1, B), jnp.float32, 0.0, math.log(10.0)))
    owners = jax.random.permutation(jax.random.fold_in(key, 22), blocks)
    target = owners[jnp.arange(B, dtype=jnp.int32) % blocks]
    owner_row = jnp.arange(M, dtype=jnp.int32) // M_DEV
    factor = jnp.where(owner_row[:, None] == target[None, :], high, rest)
    return (0.036 * mixed * row_scale * col_scale * factor, row_scale)


def draw_old_basis(key, part):

    def one_column(column):
        return basis_column(key, column).astype(jnp.bfloat16)
    columns = lax.map(one_column, jnp.arange(K, dtype=jnp.int32))
    return columns.T


def draw_new_atoms(key, part):
    new_part, row_scale = fresh_atoms(key)
    picks = jax.random.randint(jax.random.fold_in(key, 31), (3, B), 0, K)
    signs = (jax.random.randint(jax.random.fold_in(key, 32), (3, B), 0, 2) * 2 - 1).astype(jnp.float32)
    amounts = jax.random.uniform(jax.random.fold_in(key, 33), (3, B), jnp.float32, 0.5, 1.0) * signs

    def one_column(column):
        return basis_column(key, column).astype(jnp.bfloat16).astype(jnp.float32)
    chosen = lax.map(one_column, picks.reshape(-1)).reshape(3, B, M)
    coherent = jnp.sum(chosen * amounts[:, :, None], axis=0)
    return (coherent.T + new_part).astype(jnp.bfloat16)


def draw_user_residuals(key, part):
    new_part, row_scale = fresh_atoms(key)
    picks = jax.random.randint(jax.random.fold_in(key, 41), (2, U), 0, B)
    signs = (jax.random.randint(jax.random.fold_in(key, 42), (2, U), 0, 2) * 2 - 1).astype(jnp.float32)
    amounts = jax.random.uniform(jax.random.fold_in(key, 43), (2, U), jnp.float32, 1.0, 2.0) * signs
    combined = jnp.take(new_part, picks[0], axis=1) * amounts[0][None, :] + jnp.take(new_part, picks[1], axis=1) * amounts[1][None, :]
    noise = jax.random.truncated_normal(jax.random.fold_in(key, 44), -4.0, 4.0, (M, U), jnp.float32)
    return (combined + 0.5 * noise * row_scale / 4.6).astype(jnp.bfloat16)


def setup_inputs(seed: int = 0) -> dict:
    arg_keys = jax.random.split(jax.random.key(seed), 4)
    old_basis = draw_old_basis(jax.random.fold_in(arg_keys[3], 71), 0)
    new_atoms = draw_new_atoms(jax.random.fold_in(arg_keys[3], 71), 0)
    user_residuals = draw_user_residuals(jax.random.fold_in(arg_keys[3], 71), 0)
    return {"old_basis": old_basis, "new_atoms": new_atoms, "user_residuals": user_residuals}


def column_sums(old_basis, remainder_low):
    basis_blocks = old_basis.reshape(N_ROWS, M_DEV, K)
    low_blocks = remainder_low.reshape(N_ROWS, M_DEV, B)

    def add_block(running, block_pair):
        product = jnp.einsum('rk,rb->kb', block_pair[0].astype(jnp.float32), block_pair[1].astype(jnp.float32))
        return (running + product, None)
    running, unused = lax.scan(add_block, jnp.zeros((K, B), jnp.float32), (basis_blocks, low_blocks))
    return running

def finish_block(remainder_low, gram_total, coupling_total, user_residuals, m_total):
    gram_matrix = gram_total / m_total
    factor_lower = jnp.linalg.cholesky(gram_matrix)
    identity = jnp.eye(gram_matrix.shape[0], dtype=jnp.float32)
    inverse = jax.scipy.linalg.solve_triangular(factor_lower, identity, lower=True)
    new_block = jnp.dot(remainder_low.astype(jnp.float32), inverse.T, precision=lax.Precision.HIGHEST).astype(jnp.bfloat16)
    weights_low = jnp.dot(inverse, coupling_total / m_total, precision=lax.Precision.HIGHEST).astype(jnp.bfloat16)
    updated = user_residuals.astype(jnp.float32) - jnp.dot(new_block.astype(jnp.float32), weights_low.astype(jnp.float32), preferred_element_type=jnp.float32)
    return (new_block, updated.astype(jnp.bfloat16))

def reference(old_basis, new_atoms, user_residuals):
    m_total = float(M)
    remainder = new_atoms.astype(jnp.float32)
    remainder_low = new_atoms
    for sweep_index in range(2):
        coef_low = (column_sums(old_basis, remainder_low) / m_total).astype(jnp.bfloat16)
        remainder = remainder - jnp.dot(old_basis.astype(jnp.float32), coef_low.astype(jnp.float32), preferred_element_type=jnp.float32)
        remainder_low = remainder.astype(jnp.bfloat16)
    gram_total = jnp.dot(remainder_low.T.astype(jnp.float32), remainder_low.astype(jnp.float32), preferred_element_type=jnp.float32)
    coupling_total = jnp.dot(remainder_low.T.astype(jnp.float32), user_residuals.astype(jnp.float32), preferred_element_type=jnp.float32)
    return finish_block(remainder_low, gram_total, coupling_total, user_residuals, m_total)
```

```python
import functools

import jax
import jax.numpy as jnp
from jax import lax
from jax.experimental import pallas as pl
from jax.experimental.pallas import tpu as pltpu
from jax.sharding import PartitionSpec as P

BF16, F32 = jnp.bfloat16, jnp.float32
VMEM = pl.BlockSpec(memory_space=pltpu.VMEM)
SMEM = pl.BlockSpec(memory_space=pltpu.SMEM)
QUARTERS = 4
NT = (((1,), (1,)), ((), ()))
TN = (((0,), (0,)), ((), ()))


def params():
    return pltpu.CompilerParams(vmem_limit_bytes=32 * 2**20)


def swap(value, bit_of_core):
    size = lax.axis_size("rows")
    pairs = [(i, i ^ (1 << bit_of_core[i & 1])) for i in range(size)]
    return lax.ppermute(value, "rows", pairs)


def coef_kernel(places, offset_ref, basis_ref, rem_ref, *out_refs):
    width = out_refs[0].shape[2]
    turned = rem_ref[...].T
    for out_ref, first in zip(out_refs, places):
        for q in range(QUARTERS):
            start = pl.multiple_of(offset_ref[first + q], width)
            product = jnp.dot(turned, basis_ref[:, pl.ds(start, width)], preferred_element_type=F32)
            out_ref[q] = product.astype(out_ref.dtype)


def coef_call(offsets, basis, rem_low, places, width, dtype):
    block = rem_low.shape[1]
    shape = jax.ShapeDtypeStruct((QUARTERS, block, width), dtype)
    flops = 2 * basis.shape[0] * block * width * QUARTERS * len(places)
    return pl.pallas_call(
        functools.partial(coef_kernel, places),
        in_specs=[SMEM, VMEM, VMEM],
        out_specs=[VMEM] * len(places),
        out_shape=[shape] * len(places),
        compiler_params=params(),
        cost_estimate=pl.CostEstimate(flops=flops, bytes_accessed=0, transcendentals=0),
    )(offsets, basis, rem_low)


def project(places, offset_ref, basis_ref, coef_refs, total):
    for coef_ref, first in zip(coef_refs, places):
        width = coef_ref.shape[2]
        for q in range(QUARTERS):
            start = pl.multiple_of(offset_ref[first + q], width)
            total = total - lax.dot_general(
                basis_ref[:, pl.ds(start, width)], coef_ref[q], NT, preferred_element_type=F32
            )
    return total


def image_kernel(places, offset_ref, basis_ref, rem_ref, *refs):
    coef_refs, out_refs = refs[: len(places)], refs[len(places) :]
    total = project(places, offset_ref, basis_ref, coef_refs, rem_ref[...].astype(F32))
    out_refs[0][...] = total
    if len(out_refs) > 1:
        out_refs[1][...] = total.astype(BF16)


def image_call(offsets, basis, rem, coefs, places, low):
    shapes = [jax.ShapeDtypeStruct(rem.shape, F32)]
    if low:
        shapes.append(jax.ShapeDtypeStruct(rem.shape, BF16))
    flops = 2 * rem.size * coefs[0].shape[2] * QUARTERS * len(places)
    return pl.pallas_call(
        functools.partial(image_kernel, places),
        in_specs=[SMEM] + [VMEM] * (2 + len(coefs)),
        out_specs=[VMEM] * len(shapes),
        out_shape=shapes,
        compiler_params=params(),
        cost_estimate=pl.CostEstimate(flops=flops, bytes_accessed=0, transcendentals=0),
    )(offsets, basis, rem, *coefs)


def block_offsets(width, chains):
    me = lax.axis_index("rows")
    core, low, high = me & 1, (me >> 1) & 1, (me >> 2) & 1
    order = jnp.arange(QUARTERS, dtype=jnp.int32)
    turns = jnp.stack([2 * low + high, 2 * high + low])
    lists = []
    for half in (core, 1 - core):
        turn = jnp.where(half == 0, turns[0], turns[1])
        for chain in range(chains):
            lists.append((chain * 2 + half) * QUARTERS + (order ^ turn))
    return jnp.concatenate(lists).astype(jnp.int32) * width


def summed_coefs(own, other, m_total):
    bits = (lax.axis_size("rows") - 1).bit_length()
    first, second = (1, 2), (2, 1)
    chains = range(len(own))
    got = [swap(v, (0, 0)) for v in other]
    own = [own[i] + got[i] for i in chains]
    got = [swap(v[2:].astype(BF16), first) for v in own]
    own = [own[i][:2] + got[i] for i in chains]
    got = [swap(v[1:].astype(BF16), second) for v in own]
    own = [own[i][:1] + got[i] for i in chains]
    for bit in range(3, bits):
        got = [swap(v.astype(BF16), (bit, bit)) for v in own]
        own = [own[i] + got[i] for i in chains]
    own = [(v / m_total).astype(BF16) for v in own]
    got = [swap(v, second) for v in own]
    own = [jnp.concatenate([own[i], got[i]]) for i in chains]
    got = [swap(v, first) for v in own]
    own = [jnp.concatenate([own[i], got[i]]) for i in chains]
    return own, [swap(v, (0, 0)) for v in own]


def sweep(offsets, basis, rem, rem_low, width, chains, m_total):
    mine = tuple(QUARTERS * i for i in range(chains))
    others = tuple(QUARTERS * (chains + i) for i in range(chains))
    other = coef_call(offsets, basis, rem_low, others, width, BF16)
    own = coef_call(offsets, basis, rem_low, mine, width, F32)
    own, other = summed_coefs(own, other, m_total)
    for i in range(chains):
        (rem,) = image_call(offsets, basis, rem, own[i : i + 1], mine[i : i + 1], False)
    return image_call(offsets, basis, rem, other, others, True)


def plain_sweep(basis, rem, rem_low, m_total):
    partial_coef = jnp.einsum("rk,rb->kb", basis, rem_low, preferred_element_type=F32)
    coef_low = (lax.psum(partial_coef, "rows") / m_total).astype(BF16)
    image = jnp.dot(basis, coef_low, preferred_element_type=F32)
    rem = rem - lax.psum(image, "users")
    return rem, rem.astype(BF16)


def small_sums(gram_part, coupling_part):
    bits = (lax.axis_size("rows") - 1).bit_length()
    core = lax.axis_index("rows") & 1
    own = jnp.where(core == 0, gram_part, coupling_part)
    own = own + swap(jnp.where(core == 0, coupling_part, gram_part), (0, 0))
    for pair in [(1, 2), (2, 1)] + [(bit, bit) for bit in range(3, bits)]:
        own = own + swap(own, pair)
    got = swap(own, (0, 0))
    return jnp.where(core == 0, own, got), jnp.where(core == 0, got, own)


def finish_block(remainder_low, gram_total, coupling_total, user_residuals, m_total):
    gram_matrix = gram_total / m_total
    factor_lower = jnp.linalg.cholesky(gram_matrix)
    identity = jnp.eye(gram_matrix.shape[0], dtype=F32)
    inverse = jax.scipy.linalg.solve_triangular(factor_lower, identity, lower=True)
    new_block = jnp.dot(
        remainder_low.astype(F32), inverse.T, precision=lax.Precision.HIGHEST
    ).astype(BF16)
    weights_low = jnp.dot(
        inverse, coupling_total / m_total, precision=lax.Precision.HIGHEST
    ).astype(BF16)
    updated = user_residuals.astype(F32) - jnp.dot(
        new_block, weights_low, preferred_element_type=F32
    )
    return (new_block, updated.astype(BF16))


def local(old_basis, new_atoms, user_residuals):
    rows, atoms = old_basis.shape
    size = lax.axis_size("rows")
    users = lax.axis_size("users")
    m_total = float(rows * size)
    power = size >= 8 and size & (size - 1) == 0
    chains = 2 if atoms % (2 * 2 * QUARTERS * 128) == 0 else 1
    width = atoms // (chains * 2 * QUARTERS)
    paired = power and atoms % (chains * 2 * QUARTERS * 128) == 0 and rows % 128 == 0

    rem, rem_low = new_atoms.astype(F32), new_atoms
    offsets = block_offsets(width, chains) if paired else None
    for _ in range(2):
        if not paired:
            rem, rem_low = plain_sweep(old_basis, rem, rem_low, m_total)
        elif users == 1:
            rem, rem_low = sweep(offsets, old_basis, rem, rem_low, width, chains, m_total)
        else:
            image, _ = sweep(offsets, old_basis, jnp.zeros_like(rem), rem_low, width, chains, m_total)
            rem = rem + lax.psum(image, "users")
            rem_low = rem.astype(BF16)
    gram_part = lax.dot_general(rem_low, rem_low, TN, preferred_element_type=F32)
    coupling_part = lax.dot_general(rem_low, user_residuals, TN, preferred_element_type=F32)
    if power and gram_part.shape == coupling_part.shape:
        gram_total, coupling_total = small_sums(gram_part, coupling_part)
    else:
        gram_total, coupling_total = lax.psum((gram_part, coupling_part), "rows")
    return finish_block(rem_low, gram_total, coupling_total, user_residuals, m_total)


def solution(mesh):
    in_specs = (P("rows", "users"), P("rows", None), P("rows", "users"))
    out_specs = (P("rows", None), P("rows", "users"))
    return jax.shard_map(local, mesh=mesh, in_specs=in_specs, out_specs=out_specs, check_vma=False)
```

```python
import functools

import jax
import jax.numpy as jnp
from jax import lax
from jax.experimental import pallas as pl
from jax.experimental.pallas import tpu as pltpu
from jax.sharding import PartitionSpec as P

BF16, F32 = jnp.bfloat16, jnp.float32
VMEM = pl.BlockSpec(memory_space=pltpu.VMEM)
HBM = pl.BlockSpec(memory_space=pltpu.HBM)
QUARTERS = 4
NT = (((1,), (1,)), ((), ()))


def swap(value, bit_of_core):
    size = lax.axis_size("rows")
    pairs = [(i, i ^ (1 << bit_of_core[i & 1])) for i in range(size)]
    return lax.ppermute(value, "rows", pairs)


def call(kernel, shapes, flops, *operands, in_specs=None, scratch=()):
    return pl.pallas_call(
        kernel,
        in_specs=in_specs or [VMEM] * len(operands),
        out_specs=[VMEM] * len(shapes),
        out_shape=[jax.ShapeDtypeStruct(*shape) for shape in shapes],
        scratch_shapes=scratch,
        compiler_params=pltpu.CompilerParams(vmem_limit_bytes=32 * 2**20),
        cost_estimate=pl.CostEstimate(flops=flops, bytes_accessed=0, transcendentals=0),
    )(*operands)


def turns(half):
    me = lax.axis_index("rows")
    low, high = (me >> 1) & 1, (me >> 2) & 1
    return jnp.where(half == 0, 2 * low + high, 2 * high + low)


def halves():
    core = lax.axis_index("rows") & 1
    return core, 1 - core


def products(chain, swapped, rem, basis_ref, out_ref):
    width = out_ref.shape[2]
    quarter = basis_ref.shape[1] // QUARTERS
    turn = turns(halves()[swapped])
    for place in range(QUARTERS):
        start = pl.multiple_of((turn ^ place) * quarter + chain * width, width)
        product = jnp.dot(rem, basis_ref[:, pl.ds(start, width)], preferred_element_type=F32)
        out_ref[place] = product.astype(out_ref.dtype)


def load_kernel(chains, swapped, basis_ref, rows_ref, *refs):
    if not swapped:
        rem_ref, *refs = refs
    product_refs, (half_ref, kept_ref, *turned_refs, sems) = refs[:chains], refs[chains:]
    columns = half_ref.shape[1]
    start = pl.multiple_of(halves()[swapped] * columns, columns)
    copy = pltpu.make_async_copy(basis_ref.at[:, pl.ds(start, columns)], half_ref, sems.at[0])
    copy.start()
    rows_copy = pltpu.make_async_copy(rows_ref, kept_ref, sems.at[1])
    rows_copy.start()
    rows_copy.wait()
    if swapped:
        rem = kept_ref[...].T
        turned_refs[0][...] = rem
    else:
        rem = rem_ref[...]
    copy.wait()
    for chain, out_ref in enumerate(product_refs):
        products(chain, swapped, rem, half_ref, out_ref)


def load_call(swapped, basis, rows, rem, chains):
    height, atoms = basis.shape
    block = rem.shape[1] if swapped else rem.shape[0]
    width = atoms // (2 * QUARTERS * chains)
    shapes = [((QUARTERS, block, width), BF16 if swapped else F32)] * chains
    shapes += [((height, atoms // 2), BF16), (rows.shape, BF16)]
    if swapped:
        shapes.append(((block, height), BF16))
    basis, rows = (pltpu.with_memory_space_constraint(v, pltpu.HBM) for v in (basis, rows))
    kernel = functools.partial(load_kernel, chains, swapped)
    operands = [basis, rows] if swapped else [basis, rows, rem]
    specs = [HBM, HBM, VMEM][: len(operands)]
    scratch = [pltpu.SemaphoreType.DMA((2,))]
    return call(kernel, shapes, basis.size * block, *operands, in_specs=specs, scratch=scratch)


def coef_kernel(chain, swapped, basis_ref, rem_ref, out_ref):
    products(chain, swapped, rem_ref[...], basis_ref, out_ref)


def coef_call(swapped, basis, rem_low, chain, chains):
    block = rem_low.shape[0]
    width = basis.shape[1] // (QUARTERS * chains)
    kernel = functools.partial(coef_kernel, chain, swapped)
    shape = ((QUARTERS, block, width), BF16 if swapped else F32)
    return call(kernel, [shape], 2 * basis.size * block // chains, basis, rem_low)[0]


def image_kernel(chain, swapped, first, basis_ref, rem_ref, coef_ref, *out_refs):
    total = rem_ref[...].astype(F32)
    count, _, width = coef_ref.shape
    quarter = basis_ref.shape[1] // QUARTERS
    turn = turns(halves()[swapped])
    for i in range(count):
        start = pl.multiple_of((turn ^ (first + i)) * quarter + chain * width, width)
        columns = basis_ref[:, pl.ds(start, width)]
        total = total - lax.dot_general(coef_ref[i], columns, NT, preferred_element_type=F32)
    for out_ref in out_refs:
        out_ref[...] = total.astype(out_ref.dtype)


def image_call(chain, swapped, basis, rem, coef, first, dtypes):
    shapes = [(rem.shape, dtype) for dtype in dtypes]
    flops = 2 * rem.size * coef.shape[0] * coef.shape[2]
    return call(functools.partial(image_kernel, chain, swapped, first), shapes, flops, basis, rem, coef)


def sweep(own_half, other_half, rem, own, other, m_total, dtypes):
    bits = (lax.axis_size("rows") - 1).bit_length()
    chains = range(len(own))
    got = [swap(v, (0, 0)) for v in other]
    own = [own[i] + got[i] for i in chains]
    got = [swap(v[2:].astype(BF16), (1, 2)) for v in own]
    own = [own[i][:2] + got[i] for i in chains]
    got = [swap(v[1:].astype(BF16), (2, 1)) for v in own]
    own = [own[i][:1] + got[i] for i in chains]
    for bit in range(3, bits):
        got = [swap(v.astype(BF16), (bit, bit)) for v in own]
        own = [own[i] + got[i] for i in chains]
    own = [(v / m_total).astype(BF16) for v in own]
    got = [swap(v, (2, 1)) for v in own]
    near = [jnp.concatenate([own[i], got[i]]) for i in chains]
    far = [swap(v, (1, 2)) for v in near]
    other = [swap(jnp.concatenate([near[i], far[i]]), (0, 0)) for i in chains]
    for first, parts in ((0, near), (2, far)):
        for i in chains:
            (rem,) = image_call(i, False, own_half, rem, parts[i], first, [F32])
    for i in chains[:-1]:
        (rem,) = image_call(i, True, other_half, rem, other[i], 0, [F32])
    return image_call(chains[-1], True, other_half, rem, other[-1], 0, dtypes)


def plain_sweep(basis, rem, rem_low, m_total):
    coef = jnp.einsum("br,rk->bk", rem_low, basis, preferred_element_type=F32)
    coef_low = (lax.psum(coef, "rows") / m_total).astype(BF16)
    image = lax.dot_general(coef_low, basis, NT, preferred_element_type=F32)
    rem = rem - lax.psum(image, "users")
    return rem, rem.astype(BF16)


def small_kernel(turned_ref, user_ref, own_ref, other_ref, rem_ref):
    turned = turned_ref[...]
    rem = turned.T
    gram = jnp.dot(turned, rem, preferred_element_type=F32)
    coupling = jnp.dot(turned, user_ref[...], preferred_element_type=F32)
    first = (lax.axis_index("rows") & 1) == 0
    own_ref[...] = jnp.where(first, gram, coupling)
    other_ref[...] = jnp.where(first, coupling, gram)
    rem_ref[...] = rem


def small_parts(turned_low, user_residuals):
    square = ((user_residuals.shape[1],) * 2, F32)
    return call(small_kernel, [square, square, (user_residuals.shape, BF16)], 0, turned_low, user_residuals)


def small_sums(own, other):
    bits = (lax.axis_size("rows") - 1).bit_length()
    own = own + swap(other, (0, 0))
    for pair in [(1, 2), (2, 1)] + [(bit, bit) for bit in range(3, bits)]:
        own = own + swap(own, pair)
    return own, swap(own, (0, 0))


def inverse_factor(gram):
    size = gram.shape[0]
    lane = lax.broadcasted_iota(jnp.int32, (8, size), 1)
    row = lax.broadcasted_iota(jnp.int32, (8, size), 0)
    panels = [gram[8 * i : 8 * i + 8] for i in range(size // 8)]
    result = []

    def across(value, index):
        return jnp.broadcast_to(value[:, index : index + 1], (8, size))

    def down(value, index):
        return jnp.broadcast_to(value[index : index + 1], (8, size))

    for k, panel in enumerate(panels):
        inside = (lane >= 8 * k) & (lane < 8 * k + 8)
        columns = [across(panel, 8 * k + c) for c in range(8)]
        full = jnp.where(inside, (lane == row + 8 * k).astype(F32), panel)
        lower, pivots = full, columns[0]
        for s in range(8):
            pivot, line = down(columns[s], s), down(full, s)
            if s:
                lower, pivots = jnp.where(row == s, line, lower), jnp.where(row == s, pivot, pivots)
            factor = jnp.where(row == s, 0.0, columns[s] * (1.0 / pivot))
            for c in range(s + 1, 8):
                columns[c] = columns[c] - factor * down(columns[c], s)
            full = full - factor * line
        full = full * (1.0 / pivots)
        result.append(jnp.where(lane <= row + 8 * k, lower * lax.rsqrt(pivots), 0.0))
        for i in range(k + 1, size // 8):
            value = jnp.where(inside, 0.0, panels[i])
            for c in range(8):
                value = value - across(panels[i], 8 * k + c) * down(full, c)
            panels[i] = value
    return jnp.concatenate(result)


def thirds(value):
    high = value.astype(BF16)
    rest = value - high.astype(F32)
    middle = rest.astype(BF16)
    return high, middle, (rest - middle.astype(F32)).astype(BF16)


def finish_kernel(m_total, own_ref, other_ref, rem_ref, user_ref, block_ref, updated_ref):
    first = (lax.axis_index("rows") & 1) == 0
    own, other = own_ref[...], other_ref[...]
    inverse = inverse_factor(jnp.where(first, own, other) * (1.0 / m_total))
    rem = rem_ref[...]
    parts = [lax.dot_general(rem, part, NT, preferred_element_type=F32) for part in thirds(inverse)]
    block = (parts[2] + parts[1] + parts[0]).astype(BF16)
    coupling = jnp.where(first, other, own) * (1.0 / m_total)
    weights = jnp.dot(inverse, coupling, precision=lax.Precision.HIGHEST, preferred_element_type=F32)
    block_ref[...] = block
    image = jnp.dot(block, weights.astype(BF16), preferred_element_type=F32)
    updated_ref[...] = (user_ref[...].astype(F32) - image).astype(BF16)


def finish(own, other, rem_low, user_residuals, m_total):
    shapes = [(v.shape, BF16) for v in (rem_low, user_residuals)]
    return tuple(call(functools.partial(finish_kernel, m_total), shapes, 0, own, other, rem_low, user_residuals))


def plain_finish(remainder_low, gram_total, coupling_total, user_residuals, m_total):
    factor_lower = jnp.linalg.cholesky(gram_total / m_total)
    identity = jnp.eye(factor_lower.shape[0], dtype=F32)
    inverse = jax.scipy.linalg.solve_triangular(factor_lower, identity, lower=True)
    new_block = jnp.dot(remainder_low.astype(F32), inverse.T, precision=lax.Precision.HIGHEST).astype(BF16)
    weights = jnp.dot(inverse, coupling_total / m_total, precision=lax.Precision.HIGHEST).astype(BF16)
    updated = user_residuals.astype(F32) - jnp.dot(new_block, weights, preferred_element_type=F32)
    return (new_block, updated.astype(BF16))


def plain_local(old_basis, new_atoms, user_residuals):
    m_total = float(old_basis.shape[0] * lax.axis_size("rows"))
    rem, rem_low = new_atoms.T.astype(F32), new_atoms.T
    for _ in range(2):
        rem, rem_low = plain_sweep(old_basis, rem, rem_low, m_total)
    gram = lax.dot_general(rem_low, rem_low, NT, preferred_element_type=F32)
    coupling = jnp.dot(rem_low, user_residuals, preferred_element_type=F32)
    gram, coupling = lax.psum((gram, coupling), "rows")
    return plain_finish(rem_low.T, gram, coupling, user_residuals, m_total)


def local(old_basis, new_atoms, user_residuals):
    rows, atoms = old_basis.shape
    block = new_atoms.shape[1]
    size = lax.axis_size("rows")
    users = lax.axis_size("users")
    m_total = float(rows * size)
    chains = 2 if atoms % (2 * 2 * QUARTERS * 128) == 0 else 1
    power = size >= 8 and size & (size - 1) == 0
    tiled = rows % 128 == 0 and atoms % (chains * 2 * QUARTERS * 128) == 0
    if not power or not tiled or block != 128 or user_residuals.shape[1] != block:
        return plain_local(old_basis, new_atoms, user_residuals)

    *other, other_half, _, rem_low = load_call(True, old_basis, new_atoms, new_atoms, chains)
    *own, own_half, user_rows = load_call(False, old_basis, user_residuals, rem_low, chains)
    rem = rem_low
    for last in (False, True):
        if last:
            other = [coef_call(True, other_half, rem_low, i, chains) for i in range(chains)]
            own = [coef_call(False, own_half, rem_low, i, chains) for i in range(chains)]
        dtypes = [BF16] if last and users == 1 else [F32, BF16]
        start = rem if users == 1 else jnp.zeros(rem.shape, F32)
        *new, rem_low = sweep(own_half, other_half, start, own, other, m_total, dtypes)
        if users == 1:
            rem = new[0] if new else rem
        else:
            rem = rem.astype(F32) + lax.psum(new[0], "users")
            rem_low = rem.astype(BF16)
    own, other, rem_low = small_parts(rem_low, user_rows)
    own, other = small_sums(own, other)
    return finish(own, other, rem_low, user_rows, m_total)


def solution(mesh):
    in_specs = (P("rows", "users"), P("rows", None), P("rows", "users"))
    out_specs = (P("rows", None), P("rows", "users"))
    return jax.shard_map(local, mesh=mesh, in_specs=in_specs, out_specs=out_specs, check_vma=False)
```

```python
import functools

import jax
import jax.numpy as jnp
from jax import lax
from jax.experimental import pallas as pl
from jax.experimental.pallas import tpu as pltpu
from jax.sharding import PartitionSpec as P

BF16, F32 = jnp.bfloat16, jnp.float32
VMEM = pl.BlockSpec(memory_space=pltpu.VMEM)
HBM = pl.BlockSpec(memory_space=pltpu.HBM)
QUARTERS = 4
NT = (((1,), (1,)), ((), ()))


CORE = (1, 1)
SHARE = ((2, 4), (4, 2))


def summed_bits():
    bits = [1 << bit for bit in range(3, (lax.axis_size("rows") - 1).bit_length())]
    pairs = []
    while bits:
        first, second = bits[0], bits[min(1, len(bits) - 1)]
        pairs += [(first, second), (second, first)][: len(bits)]
        bits = bits[2:]
    return pairs


def place_masks(place):
    return tuple((place >> 1) * high + (place & 1) * low for high, low in SHARE)


def swap(value, masks):
    size = lax.axis_size("rows")
    return lax.ppermute(value, "rows", [(i, i ^ masks[i & 1]) for i in range(size)])


def call(kernel, shapes, flops, *operands, in_specs=None, scratch=()):
    return pl.pallas_call(
        kernel,
        in_specs=in_specs or [VMEM] * len(operands),
        out_specs=[VMEM] * len(shapes),
        out_shape=[jax.ShapeDtypeStruct(*shape) for shape in shapes],
        scratch_shapes=scratch,
        compiler_params=pltpu.CompilerParams(vmem_limit_bytes=32 * 2**20),
        cost_estimate=pl.CostEstimate(flops=flops, bytes_accessed=0, transcendentals=0),
    )(*operands)


def turns(half):
    me = lax.axis_index("rows")
    turn = [2 * jnp.where(me & high, 1, 0) + jnp.where(me & low, 1, 0) for high, low in SHARE]
    return jnp.where(half == 0, turn[0], turn[1])


def halves():
    core = lax.axis_index("rows") & 1
    return core, 1 - core


def products(swapped, places, rem, basis_ref, out_refs):
    quarter = basis_ref.shape[1] // QUARTERS
    turn = turns(halves()[swapped])
    for place, out_ref in zip(places, out_refs):
        start = pl.multiple_of((turn ^ place) * quarter, quarter)
        product = jnp.dot(rem, basis_ref[:, pl.ds(start, quarter)], preferred_element_type=F32)
        out_ref[...] = product.astype(out_ref.dtype)


def load_kernel(swapped, basis_ref, rows_ref, *refs):
    if not swapped:
        rem_ref, *refs = refs
    product_refs, (half_ref, kept_ref, *turned_refs, sems) = refs[:QUARTERS], refs[QUARTERS:]
    columns = half_ref.shape[1]
    start = pl.multiple_of(halves()[swapped] * columns, columns)
    copy = pltpu.make_async_copy(basis_ref.at[:, pl.ds(start, columns)], half_ref, sems.at[0])
    copy.start()
    rows_copy = pltpu.make_async_copy(rows_ref, kept_ref, sems.at[1])
    rows_copy.start()
    rows_copy.wait()
    if swapped:
        rem = kept_ref[...].T
        turned_refs[0][...] = rem
    else:
        rem = rem_ref[...]
    copy.wait()
    products(swapped, range(QUARTERS), rem, half_ref, product_refs)


def load_call(swapped, basis, rows, rem):
    height, atoms = basis.shape
    block = rem.shape[1] if swapped else rem.shape[0]
    shapes = [((block, atoms // (2 * QUARTERS)), BF16 if swapped else F32)] * QUARTERS
    shapes += [((height, atoms // 2), BF16), (rows.shape, BF16)]
    if swapped:
        shapes.append(((block, height), BF16))
    basis, rows = (pltpu.with_memory_space_constraint(v, pltpu.HBM) for v in (basis, rows))
    kernel = functools.partial(load_kernel, swapped)
    operands = [basis, rows] if swapped else [basis, rows, rem]
    specs = [HBM, HBM, VMEM][: len(operands)]
    scratch = [pltpu.SemaphoreType.DMA((2,))]
    return call(kernel, shapes, basis.size * block, *operands, in_specs=specs, scratch=scratch)


def coef_kernel(swapped, places, basis_ref, rem_ref, *out_refs):
    products(swapped, places, rem_ref[...], basis_ref, out_refs)


def coef_call(swapped, places, basis, rem_low):
    block = rem_low.shape[0]
    quarter = basis.shape[1] // QUARTERS
    shapes = [((block, quarter), BF16 if swapped else F32)] * len(places)
    flops = 2 * rem_low.size * quarter * len(places)
    return call(functools.partial(coef_kernel, swapped, places), shapes, flops, basis, rem_low)


def image_kernel(swapped, places, basis_ref, rem_ref, *refs):
    coef_refs, out_refs = refs[: len(places)], refs[len(places) :]
    total = rem_ref[...].astype(F32)
    quarter = basis_ref.shape[1] // QUARTERS
    turn = turns(halves()[swapped])
    for place, coef_ref in zip(places, coef_refs):
        start = pl.multiple_of((turn ^ place) * quarter, quarter)
        columns = basis_ref[:, pl.ds(start, quarter)]
        total = total - lax.dot_general(coef_ref[...], columns, NT, preferred_element_type=F32)
    for out_ref in out_refs:
        out_ref[...] = total.astype(out_ref.dtype)


def image_call(swapped, places, basis, rem, coefs, dtypes):
    shapes = [(rem.shape, dtype) for dtype in dtypes]
    flops = 2 * rem.size * coefs[0].shape[1] * len(places)
    return call(functools.partial(image_kernel, swapped, places), shapes, flops, basis, rem, *coefs)


def sweep(own_half, other_half, rem, own, other, m_total, dtypes):
    got = {place: swap(other[place], CORE) for place in (3, 2, 1, 0)}
    sent = {place: swap((own[place] + got[place]).astype(BF16), place_masks(place)) for place in (3, 2, 1)}
    total = own[0] + got[0] + sent[3] + sent[2] + sent[1]
    for masks in summed_bits():
        total = total + swap(total.astype(BF16), masks)
    coef = {0: (total / m_total).astype(BF16)}
    for place in (3, 2, 1):
        coef[place] = swap(coef[0], place_masks(place))
    other = {place: swap(coef[place], CORE) for place in (0, 3, 2, 1)}
    (rem,) = image_call(False, (0, 3), own_half, rem, [coef[0], coef[3]], [F32])
    (rem,) = image_call(True, (0, 3), other_half, rem, [other[0], other[3]], [F32])
    (rem,) = image_call(False, (2, 1), own_half, rem, [coef[2], coef[1]], [F32])
    return image_call(True, (2, 1), other_half, rem, [other[2], other[1]], dtypes)


def plain_sweep(basis, rem, rem_low, m_total):
    coef = jnp.einsum("br,rk->bk", rem_low, basis, preferred_element_type=F32)
    coef_low = (lax.psum(coef, "rows") / m_total).astype(BF16)
    image = lax.dot_general(coef_low, basis, NT, preferred_element_type=F32)
    rem = rem - lax.psum(image, "users")
    return rem, rem.astype(BF16)


def small_kernel(turned_ref, user_ref, own_ref, other_ref, rem_ref):
    turned = turned_ref[...]
    rem = turned.T
    gram = jnp.dot(turned, rem, preferred_element_type=F32)
    coupling = jnp.dot(turned, user_ref[...], preferred_element_type=F32)
    first = (lax.axis_index("rows") & 1) == 0
    own_ref[...] = jnp.where(first, gram, coupling)
    other_ref[...] = jnp.where(first, coupling, gram)
    rem_ref[...] = rem


def small_parts(turned_low, user_residuals):
    square = ((user_residuals.shape[1],) * 2, F32)
    return call(small_kernel, [square, square, (user_residuals.shape, BF16)], 0, turned_low, user_residuals)


def small_sums(own, other):
    own = own + swap(other, CORE)
    own = own + sum(swap(own, place_masks(place)) for place in (3, 2, 1))
    for masks in summed_bits():
        own = own + swap(own, masks)
    return own, swap(own, CORE)


def inverse_factor(gram):
    size = gram.shape[0]
    group = 32
    lane = lax.broadcasted_iota(jnp.int32, (8, size), 1)
    row = lax.broadcasted_iota(jnp.int32, (8, size), 0)
    panels = [gram[i : i + 8] for i in range(0, size, 8)]
    result = []

    def across(value, index):
        return jnp.broadcast_to(value[:, index : index + 1], (8, size))

    def down(value, index):
        return jnp.broadcast_to(value[index : index + 1], (8, size))

    for top in range(0, size, group):
        end = min(top + group, size)
        scaled = []
        for first in range(top, end, 8):
            panel = panels[first // 8]
            inside = (lane >= first) & (lane < first + 8)
            columns = [across(panel, first + c) for c in range(8)]
            full = jnp.where(inside, (lane == row + first).astype(F32), panel)
            lower, pivots = full, columns[0]
            for s in range(8):
                pivot, line = down(columns[s], s), down(full, s)
                if s:
                    lower, pivots = jnp.where(row == s, line, lower), jnp.where(row == s, pivot, pivots)
                factor = jnp.where(row == s, 0.0, columns[s] * (1.0 / pivot))
                for c in range(s + 1, 8):
                    columns[c] = columns[c] - factor * down(columns[c], s)
                full = full - factor * line
            full = full * (1.0 / pivots)
            lower = lower * lax.rsqrt(pivots)
            scaled.append(jnp.where((lane > row + first) & (lane < end), 0.0, lower))
            for later in range(first + 8, end, 8):
                value = panels[later // 8]
                total = jnp.where(inside, 0.0, value)
                for c in range(8):
                    total = total - across(value, first + c) * down(full, c)
                panels[later // 8] = total
        result += [jnp.where(lane < end, value, 0.0) for value in scaled]
        if end < size:
            rows = jnp.concatenate(scaled)
            update = jnp.dot(
                rows.T[end:], rows, precision=lax.Precision.HIGHEST, preferred_element_type=F32
            )
            inside = (lane >= top) & (lane < end)
            for first in range(end, size, 8):
                value = jnp.where(inside, 0.0, panels[first // 8])
                panels[first // 8] = value - update[first - end : first - end + 8]
    return jnp.concatenate(result)


def thirds(value):
    high = value.astype(BF16)
    rest = value - high.astype(F32)
    middle = rest.astype(BF16)
    return high, middle, (rest - middle.astype(F32)).astype(BF16)


def finish_kernel(m_total, own_ref, other_ref, rem_ref, user_ref, block_ref, updated_ref):
    first = (lax.axis_index("rows") & 1) == 0
    own, other = own_ref[...], other_ref[...]
    inverse = inverse_factor(jnp.where(first, own, other) * (1.0 / m_total))
    rem = rem_ref[...]
    parts = [lax.dot_general(rem, part, NT, preferred_element_type=F32) for part in thirds(inverse)]
    block = (parts[2] + parts[1] + parts[0]).astype(BF16)
    coupling = jnp.where(first, other, own) * (1.0 / m_total)
    weights = jnp.dot(inverse, coupling, precision=lax.Precision.HIGHEST, preferred_element_type=F32)
    block_ref[...] = block
    image = jnp.dot(block, weights.astype(BF16), preferred_element_type=F32)
    updated_ref[...] = (user_ref[...].astype(F32) - image).astype(BF16)


def finish(own, other, rem_low, user_residuals, m_total):
    shapes = [(v.shape, BF16) for v in (rem_low, user_residuals)]
    return tuple(call(functools.partial(finish_kernel, m_total), shapes, 0, own, other, rem_low, user_residuals))


def plain_finish(remainder_low, gram_total, coupling_total, user_residuals, m_total):
    factor_lower = jnp.linalg.cholesky(gram_total / m_total)
    identity = jnp.eye(factor_lower.shape[0], dtype=F32)
    inverse = jax.scipy.linalg.solve_triangular(factor_lower, identity, lower=True)
    new_block = jnp.dot(remainder_low.astype(F32), inverse.T, precision=lax.Precision.HIGHEST).astype(BF16)
    weights = jnp.dot(inverse, coupling_total / m_total, precision=lax.Precision.HIGHEST).astype(BF16)
    updated = user_residuals.astype(F32) - jnp.dot(new_block, weights, preferred_element_type=F32)
    return (new_block, updated.astype(BF16))


def plain_local(old_basis, new_atoms, user_residuals):
    m_total = float(old_basis.shape[0] * lax.axis_size("rows"))
    rem, rem_low = new_atoms.T.astype(F32), new_atoms.T
    for _ in range(2):
        rem, rem_low = plain_sweep(old_basis, rem, rem_low, m_total)
    gram = lax.dot_general(rem_low, rem_low, NT, preferred_element_type=F32)
    coupling = jnp.dot(rem_low, user_residuals, preferred_element_type=F32)
    gram, coupling = lax.psum((gram, coupling), "rows")
    return plain_finish(rem_low.T, gram, coupling, user_residuals, m_total)


def local(old_basis, new_atoms, user_residuals):
    rows, atoms = old_basis.shape
    block = new_atoms.shape[1]
    size = lax.axis_size("rows")
    users = lax.axis_size("users")
    m_total = float(rows * size)
    power = size >= 16 and size & (size - 1) == 0
    tiled = rows % 128 == 0 and atoms % (2 * QUARTERS * 128) == 0
    if not power or not tiled or block != 128 or user_residuals.shape[1] != block:
        return plain_local(old_basis, new_atoms, user_residuals)

    *other, other_half, _, rem_low = load_call(True, old_basis, new_atoms, new_atoms)
    *own, own_half, user_rows = load_call(False, old_basis, user_residuals, rem_low)
    rem = rem_low
    for last in (False, True):
        if last:
            last_place = coef_call(True, (3,), other_half, rem_low)
            other = coef_call(True, (0, 1, 2), other_half, rem_low) + last_place
            own = coef_call(False, (0, 1, 2, 3), own_half, rem_low)
        dtypes = [BF16] if last and users == 1 else [F32, BF16]
        start = rem if users == 1 else jnp.zeros(rem.shape, F32)
        *new, rem_low = sweep(own_half, other_half, start, own, other, m_total, dtypes)
        if users == 1:
            rem = new[0] if new else rem
        else:
            rem = rem.astype(F32) + lax.psum(new[0], "users")
            rem_low = rem.astype(BF16)
    own, other, rem_low = small_parts(rem_low, user_rows)
    own, other = small_sums(own, other)
    return finish(own, other, rem_low, user_rows, m_total)


def solution(mesh):
    in_specs = (P("rows", "users"), P("rows", None), P("rows", "users"))
    out_specs = (P("rows", None), P("rows", "users"))
    return jax.shard_map(local, mesh=mesh, in_specs=in_specs, out_specs=out_specs, check_vma=False)
```

```python
import functools

import jax
import jax.numpy as jnp
from jax import lax
from jax.experimental import pallas as pl
from jax.experimental.pallas import tpu as pltpu
from jax.sharding import PartitionSpec as P

BF16, F32 = jnp.bfloat16, jnp.float32
VMEM = pl.BlockSpec(memory_space=pltpu.VMEM)
HBM = pl.BlockSpec(memory_space=pltpu.HBM)
QUARTERS = 4
NT = (((1,), (1,)), ((), ()))


CORE = (1, 1)
SHARE = ((2, 4), (4, 2))


def summed_bits():
    bits = [1 << bit for bit in range(3, (lax.axis_size("rows") - 1).bit_length())]
    pairs = []
    while bits:
        first, second = bits[0], bits[min(1, len(bits) - 1)]
        pairs += [(first, second), (second, first)][: len(bits)]
        bits = bits[2:]
    return pairs


def place_masks(place):
    return tuple((place >> 1) * high + (place & 1) * low for high, low in SHARE)


def swap(value, masks):
    size = lax.axis_size("rows")
    return lax.ppermute(value, "rows", [(i, i ^ masks[i & 1]) for i in range(size)])


def call(kernel, shapes, flops, *operands, in_specs=None, scratch=()):
    return pl.pallas_call(
        kernel,
        in_specs=in_specs or [VMEM] * len(operands),
        out_specs=[VMEM] * len(shapes),
        out_shape=[jax.ShapeDtypeStruct(*shape) for shape in shapes],
        scratch_shapes=scratch,
        compiler_params=pltpu.CompilerParams(vmem_limit_bytes=32 * 2**20),
        cost_estimate=pl.CostEstimate(flops=flops, bytes_accessed=0, transcendentals=0),
    )(*operands)


def turns(half):
    me = lax.axis_index("rows")
    turn = [2 * jnp.where(me & high, 1, 0) + jnp.where(me & low, 1, 0) for high, low in SHARE]
    return jnp.where(half == 0, turn[0], turn[1])


def halves():
    core = lax.axis_index("rows") & 1
    return core, 1 - core


def products(swapped, places, rem, basis_ref, out_refs):
    quarter = basis_ref.shape[1] // QUARTERS
    turn = turns(halves()[swapped])
    for place, out_ref in zip(places, out_refs):
        start = pl.multiple_of((turn ^ place) * quarter, quarter)
        product = jnp.dot(rem, basis_ref[:, pl.ds(start, quarter)], preferred_element_type=F32)
        out_ref[...] = product.astype(out_ref.dtype)


def load_kernel(basis_ref, atoms_ref, user_ref, *refs):
    other_refs, own_refs, refs = refs[:QUARTERS], refs[QUARTERS : 2 * QUARTERS], refs[2 * QUARTERS :]
    other_half_ref, own_half_ref, user_rows_ref, turned_ref, rows_ref, sems = refs
    own, other = halves()

    def half_copy(half, half_ref, sem):
        columns = half_ref.shape[1]
        start = pl.multiple_of(half * columns, columns)
        return pltpu.make_async_copy(basis_ref.at[:, pl.ds(start, columns)], half_ref, sem)

    copies = [
        pltpu.make_async_copy(atoms_ref, rows_ref, sems.at[0]),
        half_copy(other, other_half_ref, sems.at[1]),
        half_copy(own, own_half_ref, sems.at[2]),
        pltpu.make_async_copy(user_ref, user_rows_ref, sems.at[3]),
    ]
    for copy in copies:
        copy.start()
    copies[0].wait()
    rem = rows_ref[...].T
    turned_ref[...] = rem
    copies[1].wait()
    products(1, range(QUARTERS), rem, other_half_ref, other_refs)
    copies[2].wait()
    products(0, range(QUARTERS), rem, own_half_ref, own_refs)
    copies[3].wait()


def first_products(basis, atoms, user_residuals):
    rows, count = basis.shape
    block = atoms.shape[1]
    product = (block, count // (2 * QUARTERS))
    half = ((rows, count // 2), BF16)
    shapes = [(product, BF16)] * QUARTERS + [(product, F32)] * QUARTERS
    shapes += [half, half, (user_residuals.shape, BF16), ((block, rows), BF16)]
    arrays = [pltpu.with_memory_space_constraint(v, pltpu.HBM) for v in (basis, atoms, user_residuals)]
    results = call(
        load_kernel,
        shapes,
        2 * atoms.size * count,
        *arrays,
        in_specs=[HBM] * 3,
        scratch=[pltpu.VMEM(atoms.shape, BF16), pltpu.SemaphoreType.DMA((4,))],
    )
    return results[:QUARTERS], results[QUARTERS : 2 * QUARTERS], *results[2 * QUARTERS :]


def coef_kernel(swapped, places, basis_ref, rem_ref, *out_refs):
    products(swapped, places, rem_ref[...], basis_ref, out_refs)


def coef_call(swapped, places, basis, rem_low):
    block = rem_low.shape[0]
    quarter = basis.shape[1] // QUARTERS
    shapes = [((block, quarter), BF16 if swapped else F32)] * len(places)
    flops = 2 * rem_low.size * quarter * len(places)
    return call(functools.partial(coef_kernel, swapped, places), shapes, flops, basis, rem_low)


def image_kernel(swapped, places, basis_ref, rem_ref, *refs):
    coef_refs, out_refs = refs[: len(places)], refs[len(places) :]
    total = rem_ref[...].astype(F32)
    quarter = basis_ref.shape[1] // QUARTERS
    turn = turns(halves()[swapped])
    for place, coef_ref in zip(places, coef_refs):
        start = pl.multiple_of((turn ^ place) * quarter, quarter)
        columns = basis_ref[:, pl.ds(start, quarter)]
        total = total - lax.dot_general(coef_ref[...], columns, NT, preferred_element_type=F32)
    for out_ref in out_refs:
        out_ref[...] = total.astype(out_ref.dtype)


def image_call(swapped, places, basis, rem, coefs, dtypes):
    shapes = [(rem.shape, dtype) for dtype in dtypes]
    flops = 2 * rem.size * coefs[0].shape[1] * len(places)
    return call(functools.partial(image_kernel, swapped, places), shapes, flops, basis, rem, *coefs)


def sweep(own_half, other_half, rem, own, other, m_total, dtypes):
    got = {place: swap(other[place], CORE) for place in (3, 2, 1, 0)}
    sent = {place: swap((own[place] + got[place]).astype(BF16), place_masks(place)) for place in (3, 2, 1)}
    total = own[0] + got[0] + sent[3] + sent[2] + sent[1]
    for masks in summed_bits():
        total = total + swap(total.astype(BF16), masks)
    coef = {0: (total / m_total).astype(BF16)}
    for place in (3, 2, 1):
        coef[place] = swap(coef[0], place_masks(place))
    other = {place: swap(coef[place], CORE) for place in (0, 3, 2, 1)}
    (rem,) = image_call(False, (0, 3), own_half, rem, [coef[0], coef[3]], [F32])
    (rem,) = image_call(True, (0, 3), other_half, rem, [other[0], other[3]], [F32])
    (rem,) = image_call(False, (2, 1), own_half, rem, [coef[2], coef[1]], [F32])
    return image_call(True, (2, 1), other_half, rem, [other[2], other[1]], dtypes)


def plain_sweep(basis, rem, rem_low, m_total):
    coef = jnp.einsum("br,rk->bk", rem_low, basis, preferred_element_type=F32)
    coef_low = (lax.psum(coef, "rows") / m_total).astype(BF16)
    image = lax.dot_general(coef_low, basis, NT, preferred_element_type=F32)
    rem = rem - lax.psum(image, "users")
    return rem, rem.astype(BF16)


def small_kernel(turned_ref, user_ref, own_ref, other_ref, rem_ref):
    turned = turned_ref[...]
    rem = turned.T
    gram = jnp.dot(turned, rem, preferred_element_type=F32)
    coupling = jnp.dot(turned, user_ref[...], preferred_element_type=F32)
    first = (lax.axis_index("rows") & 1) == 0
    own_ref[...] = jnp.where(first, gram, coupling)
    other_ref[...] = jnp.where(first, coupling, gram)
    rem_ref[...] = rem


def small_parts(turned_low, user_residuals):
    square = ((user_residuals.shape[1],) * 2, F32)
    return call(small_kernel, [square, square, (user_residuals.shape, BF16)], 0, turned_low, user_residuals)


def small_sums(own, other):
    own = own + swap(other, CORE)
    own = own + sum(swap(own, place_masks(place)) for place in (3, 2, 1))
    for masks in summed_bits():
        own = own + swap(own, masks)
    return own, swap(own, CORE)


def inverse_factor(gram):
    size = gram.shape[0]
    group = 32
    lane = lax.broadcasted_iota(jnp.int32, (8, size), 1)
    row = lax.broadcasted_iota(jnp.int32, (8, size), 0)
    panels = [gram[i : i + 8] for i in range(0, size, 8)]
    result = []

    def across(value, index):
        return jnp.broadcast_to(value[:, index : index + 1], (8, size))

    def down(value, index):
        return jnp.broadcast_to(value[index : index + 1], (8, size))

    for top in range(0, size, group):
        end = min(top + group, size)
        scaled = []
        for first in range(top, end, 8):
            panel = panels[first // 8]
            inside = (lane >= first) & (lane < first + 8)
            columns = [across(panel, first + c) for c in range(8)]
            full = jnp.where(inside, (lane == row + first).astype(F32), panel)
            lower, pivots = full, columns[0]
            for s in range(8):
                pivot, line = down(columns[s], s), down(full, s)
                if s:
                    lower, pivots = jnp.where(row == s, line, lower), jnp.where(row == s, pivot, pivots)
                factor = jnp.where(row == s, 0.0, columns[s] * (1.0 / pivot))
                for c in range(s + 1, 8):
                    columns[c] = columns[c] - factor * down(columns[c], s)
                full = full - factor * line
            full = full * (1.0 / pivots)
            lower = lower * lax.rsqrt(pivots)
            scaled.append(jnp.where((lane > row + first) & (lane < end), 0.0, lower))
            for later in range(first + 8, end, 8):
                value = panels[later // 8]
                total = jnp.where(inside, 0.0, value)
                for c in range(8):
                    total = total - across(value, first + c) * down(full, c)
                panels[later // 8] = total
        result += [jnp.where(lane < end, value, 0.0) for value in scaled]
        if end < size:
            rows = jnp.concatenate(scaled)
            update = jnp.dot(
                rows.T[end:], rows, precision=lax.Precision.HIGHEST, preferred_element_type=F32
            )
            inside = (lane >= top) & (lane < end)
            for first in range(end, size, 8):
                value = jnp.where(inside, 0.0, panels[first // 8])
                panels[first // 8] = value - update[first - end : first - end + 8]
    return jnp.concatenate(result)


def thirds(value):
    high = value.astype(BF16)
    rest = value - high.astype(F32)
    middle = rest.astype(BF16)
    return high, middle, (rest - middle.astype(F32)).astype(BF16)


def finish_kernel(m_total, own_ref, other_ref, rem_ref, user_ref, block_ref, updated_ref):
    first = (lax.axis_index("rows") & 1) == 0
    own, other = own_ref[...], other_ref[...]
    inverse = inverse_factor(jnp.where(first, own, other) * (1.0 / m_total))
    rem = rem_ref[...]
    parts = [lax.dot_general(rem, part, NT, preferred_element_type=F32) for part in thirds(inverse)]
    block = (parts[2] + parts[1] + parts[0]).astype(BF16)
    coupling = jnp.where(first, other, own) * (1.0 / m_total)
    weights = jnp.dot(inverse, coupling, precision=lax.Precision.HIGHEST, preferred_element_type=F32)
    block_ref[...] = block
    image = jnp.dot(block, weights.astype(BF16), preferred_element_type=F32)
    updated_ref[...] = (user_ref[...].astype(F32) - image).astype(BF16)


def finish(own, other, rem_low, user_residuals, m_total):
    shapes = [(v.shape, BF16) for v in (rem_low, user_residuals)]
    return tuple(call(functools.partial(finish_kernel, m_total), shapes, 0, own, other, rem_low, user_residuals))


def plain_finish(remainder_low, gram_total, coupling_total, user_residuals, m_total):
    factor_lower = jnp.linalg.cholesky(gram_total / m_total)
    identity = jnp.eye(factor_lower.shape[0], dtype=F32)
    inverse = jax.scipy.linalg.solve_triangular(factor_lower, identity, lower=True)
    new_block = jnp.dot(remainder_low.astype(F32), inverse.T, precision=lax.Precision.HIGHEST).astype(BF16)
    weights = jnp.dot(inverse, coupling_total / m_total, precision=lax.Precision.HIGHEST).astype(BF16)
    updated = user_residuals.astype(F32) - jnp.dot(new_block, weights, preferred_element_type=F32)
    return (new_block, updated.astype(BF16))


def plain_local(old_basis, new_atoms, user_residuals):
    m_total = float(old_basis.shape[0] * lax.axis_size("rows"))
    rem, rem_low = new_atoms.T.astype(F32), new_atoms.T
    for _ in range(2):
        rem, rem_low = plain_sweep(old_basis, rem, rem_low, m_total)
    gram = lax.dot_general(rem_low, rem_low, NT, preferred_element_type=F32)
    coupling = jnp.dot(rem_low, user_residuals, preferred_element_type=F32)
    gram, coupling = lax.psum((gram, coupling), "rows")
    return plain_finish(rem_low.T, gram, coupling, user_residuals, m_total)


def local(old_basis, new_atoms, user_residuals):
    rows, atoms = old_basis.shape
    block = new_atoms.shape[1]
    size = lax.axis_size("rows")
    users = lax.axis_size("users")
    m_total = float(rows * size)
    power = size >= 16 and size & (size - 1) == 0
    tiled = rows % 128 == 0 and atoms % (2 * QUARTERS * 128) == 0
    if not power or not tiled or block != 128 or user_residuals.shape[1] != block:
        return plain_local(old_basis, new_atoms, user_residuals)

    other, own, other_half, own_half, user_rows, rem_low = first_products(old_basis, new_atoms, user_residuals)
    rem = rem_low
    for last in (False, True):
        if last:
            last_place = coef_call(True, (3,), other_half, rem_low)
            other = coef_call(True, (0, 1, 2), other_half, rem_low) + last_place
            own = coef_call(False, (0, 1, 2, 3), own_half, rem_low)
        dtypes = [BF16] if last and users == 1 else [F32, BF16]
        start = rem if users == 1 else jnp.zeros(rem.shape, F32)
        *new, rem_low = sweep(own_half, other_half, start, own, other, m_total, dtypes)
        if users == 1:
            rem = new[0] if new else rem
        else:
            rem = rem.astype(F32) + lax.psum(new[0], "users")
            rem_low = rem.astype(BF16)
    own, other, rem_low = small_parts(rem_low, user_rows)
    own, other = small_sums(own, other)
    return finish(own, other, rem_low, user_rows, m_total)


def solution(mesh):
    in_specs = (P("rows", "users"), P("rows", None), P("rows", "users"))
    out_specs = (P("rows", None), P("rows", "users"))
    return jax.shard_map(local, mesh=mesh, in_specs=in_specs, out_specs=out_specs, check_vma=False)
```

```python
import functools

import jax
import jax.numpy as jnp
from jax import lax
from jax.experimental import pallas as pl
from jax.experimental.pallas import tpu as pltpu
from jax.sharding import PartitionSpec as P

BF16, F32 = jnp.bfloat16, jnp.float32
VMEM = pl.BlockSpec(memory_space=pltpu.VMEM)
HBM = pl.BlockSpec(memory_space=pltpu.HBM)
QUARTERS = 4
NT = (((1,), (1,)), ((), ()))


CORE = (1, 1)
SHARE = ((2, 4), (8, 2))


def later_bits(first):
    return [1 << bit for bit in range(first, (lax.axis_size("rows") - 1).bit_length())]


def quarter_masks():
    return [(8, 16), (16, 4)] + [(bit, bit) for bit in later_bits(5)]


def small_masks():
    bits = later_bits(3)
    groups = [[(6, 6), (2, 4), (4, 2)]]
    while bits:
        low, high = bits[0], sum(bits[1:2])
        groups.append([(mask, mask) for mask in ((high, high | low, low) if high else (low,))])
        bits = bits[2:]
    return groups


def place_masks(place):
    return tuple((place >> 1) * high + (place & 1) * low for high, low in SHARE)


def swap(value, masks):
    size = lax.axis_size("rows")
    return lax.ppermute(value, "rows", [(i, i ^ masks[i & 1]) for i in range(size)])


def call(kernel, shapes, flops, *operands, in_specs=None, scratch=()):
    return pl.pallas_call(
        kernel,
        in_specs=in_specs or [VMEM] * len(operands),
        out_specs=[VMEM] * len(shapes),
        out_shape=[jax.ShapeDtypeStruct(*shape) for shape in shapes],
        scratch_shapes=scratch,
        compiler_params=pltpu.CompilerParams(vmem_limit_bytes=32 * 2**20),
        cost_estimate=pl.CostEstimate(flops=flops, bytes_accessed=0, transcendentals=0),
    )(*operands)


def turns(half):
    me = lax.axis_index("rows")
    turn = [2 * jnp.where(me & high, 1, 0) + jnp.where(me & low, 1, 0) for high, low in SHARE]
    return jnp.where(half == 0, turn[0], turn[1])


def halves():
    core = lax.axis_index("rows") & 1
    return core, 1 - core


def products(swapped, places, rem, basis_ref, out_refs):
    quarter = basis_ref.shape[1] // QUARTERS
    turn = turns(halves()[swapped])
    for place, out_ref in zip(places, out_refs):
        start = pl.multiple_of((turn ^ place) * quarter, quarter)
        product = jnp.dot(rem, basis_ref[:, pl.ds(start, quarter)], preferred_element_type=F32)
        out_ref[...] = product.astype(out_ref.dtype)


def load_kernel(basis_ref, atoms_ref, user_ref, *refs):
    other_refs, own_refs, refs = refs[:QUARTERS], refs[QUARTERS : 2 * QUARTERS], refs[2 * QUARTERS :]
    other_half_ref, own_half_ref, user_rows_ref, turned_ref, rows_ref, sems = refs
    own, other = halves()

    def half_copy(half, half_ref, sem):
        columns = half_ref.shape[1]
        start = pl.multiple_of(half * columns, columns)
        return pltpu.make_async_copy(basis_ref.at[:, pl.ds(start, columns)], half_ref, sem)

    copies = [
        pltpu.make_async_copy(atoms_ref, rows_ref, sems.at[0]),
        half_copy(other, other_half_ref, sems.at[1]),
        half_copy(own, own_half_ref, sems.at[2]),
        pltpu.make_async_copy(user_ref, user_rows_ref, sems.at[3]),
    ]
    for copy in copies:
        copy.start()
    copies[0].wait()
    rem = rows_ref[...].T
    turned_ref[...] = rem
    copies[1].wait()
    products(1, range(QUARTERS), rem, other_half_ref, other_refs)
    copies[2].wait()
    products(0, range(QUARTERS), rem, own_half_ref, own_refs)
    copies[3].wait()


def first_products(basis, atoms, user_residuals):
    rows, count = basis.shape
    block = atoms.shape[1]
    product = (block, count // (2 * QUARTERS))
    half = ((rows, count // 2), BF16)
    shapes = [(product, BF16)] * QUARTERS + [(product, F32)] * QUARTERS
    shapes += [half, half, (user_residuals.shape, BF16), ((block, rows), BF16)]
    arrays = [pltpu.with_memory_space_constraint(v, pltpu.HBM) for v in (basis, atoms, user_residuals)]
    results = call(
        load_kernel,
        shapes,
        2 * atoms.size * count,
        *arrays,
        in_specs=[HBM] * 3,
        scratch=[pltpu.VMEM(atoms.shape, BF16), pltpu.SemaphoreType.DMA((4,))],
    )
    return results[:QUARTERS], results[QUARTERS : 2 * QUARTERS], *results[2 * QUARTERS :]


def coef_kernel(swapped, places, basis_ref, rem_ref, *out_refs):
    products(swapped, places, rem_ref[...], basis_ref, out_refs)


def coef_call(swapped, places, basis, rem_low):
    block = rem_low.shape[0]
    quarter = basis.shape[1] // QUARTERS
    shapes = [((block, quarter), BF16 if swapped else F32)] * len(places)
    flops = 2 * rem_low.size * quarter * len(places)
    return call(functools.partial(coef_kernel, swapped, places), shapes, flops, basis, rem_low)


def image_kernel(swapped, places, basis_ref, rem_ref, *refs):
    coef_refs, out_refs = refs[: len(places)], refs[len(places) :]
    total = rem_ref[...].astype(F32)
    quarter = basis_ref.shape[1] // QUARTERS
    turn = turns(halves()[swapped])
    for place, coef_ref in zip(places, coef_refs):
        start = pl.multiple_of((turn ^ place) * quarter, quarter)
        columns = basis_ref[:, pl.ds(start, quarter)]
        total = total - lax.dot_general(coef_ref[...], columns, NT, preferred_element_type=F32)
    for out_ref in out_refs:
        out_ref[...] = total.astype(out_ref.dtype)


def image_call(swapped, places, basis, rem, coefs, dtypes):
    shapes = [(rem.shape, dtype) for dtype in dtypes]
    flops = 2 * rem.size * coefs[0].shape[1] * len(places)
    return call(functools.partial(image_kernel, swapped, places), shapes, flops, basis, rem, *coefs)


def sweep(own_half, other_half, rem, own, other, m_total, dtypes):
    got = {place: swap(other[place], CORE) for place in (3, 2, 1, 0)}
    sent = {place: swap((own[place] + got[place]).astype(BF16), place_masks(place)) for place in (3, 2, 1)}
    total = own[0] + got[0] + sent[3] + sent[2] + sent[1]
    for masks in quarter_masks():
        total = total + swap(total.astype(BF16), masks)
    coef = {0: (total / m_total).astype(BF16)}
    for place in (3, 2, 1):
        coef[place] = swap(coef[0], place_masks(place))
    other = {place: swap(coef[place], CORE) for place in (0, 3, 2, 1)}
    (rem,) = image_call(False, (0, 3), own_half, rem, [coef[0], coef[3]], [F32])
    (rem,) = image_call(True, (0, 3), other_half, rem, [other[0], other[3]], [F32])
    (rem,) = image_call(False, (2, 1), own_half, rem, [coef[2], coef[1]], [F32])
    return image_call(True, (2, 1), other_half, rem, [other[2], other[1]], dtypes)


def plain_sweep(basis, rem, rem_low, m_total):
    coef = jnp.einsum("br,rk->bk", rem_low, basis, preferred_element_type=F32)
    coef_low = (lax.psum(coef, "rows") / m_total).astype(BF16)
    image = lax.dot_general(coef_low, basis, NT, preferred_element_type=F32)
    rem = rem - lax.psum(image, "users")
    return rem, rem.astype(BF16)


def small_kernel(turned_ref, user_ref, own_ref, other_ref, rem_ref):
    turned = turned_ref[...]
    rem = turned.T
    gram = jnp.dot(turned, rem, preferred_element_type=F32)
    coupling = jnp.dot(turned, user_ref[...], preferred_element_type=F32)
    first = (lax.axis_index("rows") & 1) == 0
    own_ref[...] = jnp.where(first, gram, coupling)
    other_ref[...] = jnp.where(first, coupling, gram)
    rem_ref[...] = rem


def small_parts(turned_low, user_residuals):
    square = ((user_residuals.shape[1],) * 2, F32)
    return call(small_kernel, [square, square, (user_residuals.shape, BF16)], 0, turned_low, user_residuals)


def small_sums(own, other):
    own = own + swap(other, CORE)
    for group in small_masks():
        own = own + sum(swap(own, masks) for masks in group)
    return own, swap(own, CORE)


def inverse_factor(gram):
    size = gram.shape[0]
    group = 32
    lane = lax.broadcasted_iota(jnp.int32, (8, size), 1)
    row = lax.broadcasted_iota(jnp.int32, (8, size), 0)
    panels = [gram[i : i + 8] for i in range(0, size, 8)]
    result = []

    def across(value, index):
        return jnp.broadcast_to(value[:, index : index + 1], (8, size))

    def down(value, index):
        return jnp.broadcast_to(value[index : index + 1], (8, size))

    for top in range(0, size, group):
        end = min(top + group, size)
        scaled = []
        for first in range(top, end, 8):
            panel = panels[first // 8]
            inside = (lane >= first) & (lane < first + 8)
            columns = [across(panel, first + c) for c in range(8)]
            full = jnp.where(inside, (lane == row + first).astype(F32), panel)
            lower, pivots = full, columns[0]
            for s in range(8):
                pivot, line = down(columns[s], s), down(full, s)
                if s:
                    lower, pivots = jnp.where(row == s, line, lower), jnp.where(row == s, pivot, pivots)
                factor = jnp.where(row == s, 0.0, columns[s] * (1.0 / pivot))
                for c in range(s + 1, 8):
                    columns[c] = columns[c] - factor * down(columns[c], s)
                full = full - factor * line
            full = full * (1.0 / pivots)
            lower = lower * lax.rsqrt(pivots)
            scaled.append(jnp.where((lane > row + first) & (lane < end), 0.0, lower))
            for later in range(first + 8, end, 8):
                value = panels[later // 8]
                total = jnp.where(inside, 0.0, value)
                for c in range(8):
                    total = total - across(value, first + c) * down(full, c)
                panels[later // 8] = total
        result += [jnp.where(lane < end, value, 0.0) for value in scaled]
        if end < size:
            rows = jnp.concatenate(scaled)
            update = jnp.dot(
                rows.T[end:], rows, precision=lax.Precision.HIGHEST, preferred_element_type=F32
            )
            inside = (lane >= top) & (lane < end)
            for first in range(end, size, 8):
                value = jnp.where(inside, 0.0, panels[first // 8])
                panels[first // 8] = value - update[first - end : first - end + 8]
    return jnp.concatenate(result)


def thirds(value):
    high = value.astype(BF16)
    rest = value - high.astype(F32)
    middle = rest.astype(BF16)
    return high, middle, (rest - middle.astype(F32)).astype(BF16)


def finish_kernel(m_total, own_ref, other_ref, rem_ref, user_ref, block_ref, updated_ref):
    first = (lax.axis_index("rows") & 1) == 0
    own, other = own_ref[...], other_ref[...]
    inverse = inverse_factor(jnp.where(first, own, other) * (1.0 / m_total))
    rem = rem_ref[...]
    parts = [lax.dot_general(rem, part, NT, preferred_element_type=F32) for part in thirds(inverse)]
    block = (parts[2] + parts[1] + parts[0]).astype(BF16)
    coupling = jnp.where(first, other, own) * (1.0 / m_total)
    weights = jnp.dot(inverse, coupling, precision=lax.Precision.HIGHEST, preferred_element_type=F32)
    block_ref[...] = block
    image = jnp.dot(block, weights.astype(BF16), preferred_element_type=F32)
    updated_ref[...] = (user_ref[...].astype(F32) - image).astype(BF16)


def finish(own, other, rem_low, user_residuals, m_total):
    shapes = [(v.shape, BF16) for v in (rem_low, user_residuals)]
    return tuple(call(functools.partial(finish_kernel, m_total), shapes, 0, own, other, rem_low, user_residuals))


def plain_finish(remainder_low, gram_total, coupling_total, user_residuals, m_total):
    factor_lower = jnp.linalg.cholesky(gram_total / m_total)
    identity = jnp.eye(factor_lower.shape[0], dtype=F32)
    inverse = jax.scipy.linalg.solve_triangular(factor_lower, identity, lower=True)
    new_block = jnp.dot(remainder_low.astype(F32), inverse.T, precision=lax.Precision.HIGHEST).astype(BF16)
    weights = jnp.dot(inverse, coupling_total / m_total, precision=lax.Precision.HIGHEST).astype(BF16)
    updated = user_residuals.astype(F32) - jnp.dot(new_block, weights, preferred_element_type=F32)
    return (new_block, updated.astype(BF16))


def plain_local(old_basis, new_atoms, user_residuals):
    m_total = float(old_basis.shape[0] * lax.axis_size("rows"))
    rem, rem_low = new_atoms.T.astype(F32), new_atoms.T
    for _ in range(2):
        rem, rem_low = plain_sweep(old_basis, rem, rem_low, m_total)
    gram = lax.dot_general(rem_low, rem_low, NT, preferred_element_type=F32)
    coupling = jnp.dot(rem_low, user_residuals, preferred_element_type=F32)
    gram, coupling = lax.psum((gram, coupling), "rows")
    return plain_finish(rem_low.T, gram, coupling, user_residuals, m_total)


def local(old_basis, new_atoms, user_residuals):
    rows, atoms = old_basis.shape
    block = new_atoms.shape[1]
    size = lax.axis_size("rows")
    users = lax.axis_size("users")
    m_total = float(rows * size)
    power = size >= 32 and size & (size - 1) == 0
    tiled = rows % 128 == 0 and atoms % (2 * QUARTERS * 128) == 0
    if not power or not tiled or block != 128 or user_residuals.shape[1] != block:
        return plain_local(old_basis, new_atoms, user_residuals)

    other, own, other_half, own_half, user_rows, rem_low = first_products(old_basis, new_atoms, user_residuals)
    rem = rem_low
    for last in (False, True):
        if last:
            last_place = coef_call(True, (3,), other_half, rem_low)
            other = coef_call(True, (0, 1, 2), other_half, rem_low) + last_place
            own = coef_call(False, (0, 1, 2, 3), own_half, rem_low)
        dtypes = [BF16] if last and users == 1 else [F32, BF16]
        start = rem if users == 1 else jnp.zeros(rem.shape, F32)
        *new, rem_low = sweep(own_half, other_half, start, own, other, m_total, dtypes)
        if users == 1:
            rem = new[0] if new else rem
        else:
            rem = rem.astype(F32) + lax.psum(new[0], "users")
            rem_low = rem.astype(BF16)
    own, other, rem_low = small_parts(rem_low, user_rows)
    own, other = small_sums(own, other)
    return finish(own, other, rem_low, user_rows, m_total)


def solution(mesh):
    in_specs = (P("rows", "users"), P("rows", None), P("rows", "users"))
    out_specs = (P("rows", None), P("rows", "users"))
    return jax.shard_map(local, mesh=mesh, in_specs=in_specs, out_specs=out_specs, check_vma=False)
```

```python
import functools

import jax
import jax.numpy as jnp
from jax import lax
from jax.experimental import pallas as pl
from jax.experimental.pallas import tpu as pltpu
from jax.sharding import PartitionSpec as P

BF16, F32 = jnp.bfloat16, jnp.float32
VMEM = pl.BlockSpec(memory_space=pltpu.VMEM)
HBM = pl.BlockSpec(memory_space=pltpu.HBM)
QUARTERS = 4
NT = (((1,), (1,)), ((), ()))


CORE = (1, 1)
SHARE = ((2, 4), (8, 2))


def later_bits(first):
    return [1 << bit for bit in range(first, (lax.axis_size("rows") - 1).bit_length())]


def quarter_masks():
    return [(8, 16), (16, 4)] + [(bit, bit) for bit in later_bits(5)]


def small_masks():
    bits = later_bits(3)
    groups = [[(6, 6), (2, 4), (4, 2)]]
    while bits:
        low, high = bits[0], sum(bits[1:2])
        groups.append([(mask, mask) for mask in ((high, high | low, low) if high else (low,))])
        bits = bits[2:]
    return groups


def place_masks(place):
    return tuple((place >> 1) * high + (place & 1) * low for high, low in SHARE)


def swap(value, masks):
    size = lax.axis_size("rows")
    return lax.ppermute(value, "rows", [(i, i ^ masks[i & 1]) for i in range(size)])


def call(kernel, shapes, flops, *operands, in_specs=None, scratch=()):
    return pl.pallas_call(
        kernel,
        in_specs=in_specs or [VMEM] * len(operands),
        out_specs=[VMEM] * len(shapes),
        out_shape=[jax.ShapeDtypeStruct(*shape) for shape in shapes],
        scratch_shapes=scratch,
        compiler_params=pltpu.CompilerParams(vmem_limit_bytes=32 * 2**20),
        cost_estimate=pl.CostEstimate(flops=flops, bytes_accessed=0, transcendentals=0),
    )(*operands)


def turns(half):
    me = lax.axis_index("rows")
    turn = [2 * jnp.where(me & high, 1, 0) + jnp.where(me & low, 1, 0) for high, low in SHARE]
    return jnp.where(half == 0, turn[0], turn[1])


def halves():
    core = lax.axis_index("rows") & 1
    return core, 1 - core


def products(swapped, places, rem, basis_ref, out_refs):
    quarter = basis_ref.shape[1] // QUARTERS
    turn = turns(halves()[swapped])
    for place, out_ref in zip(places, out_refs):
        start = pl.multiple_of((turn ^ place) * quarter, quarter)
        product = jnp.dot(rem, basis_ref[:, pl.ds(start, quarter)], preferred_element_type=F32)
        out_ref[...] = product.astype(out_ref.dtype)


def load_kernel(basis_ref, atoms_ref, user_ref, *refs):
    other_refs, refs = refs[:QUARTERS], refs[QUARTERS:]
    other_half_ref, own_half_ref, user_rows_ref, turned_ref, rows_ref, sems = refs
    own, other = halves()

    def half_copy(half, half_ref, sem):
        columns = half_ref.shape[1]
        start = pl.multiple_of(half * columns, columns)
        return pltpu.make_async_copy(basis_ref.at[:, pl.ds(start, columns)], half_ref, sem)

    copies = [
        pltpu.make_async_copy(atoms_ref, rows_ref, sems.at[0]),
        half_copy(other, other_half_ref, sems.at[1]),
        half_copy(own, own_half_ref, sems.at[2]),
        pltpu.make_async_copy(user_ref, user_rows_ref, sems.at[3]),
    ]
    for copy in copies:
        copy.start()
    copies[0].wait()
    rem = rows_ref[...].T
    turned_ref[...] = rem
    copies[1].wait()
    products(1, range(QUARTERS), rem, other_half_ref, other_refs)
    for copy in copies[2:]:
        copy.wait()


def first_products(basis, atoms, user_residuals):
    rows, count = basis.shape
    block = atoms.shape[1]
    product = (block, count // (2 * QUARTERS))
    half = ((rows, count // 2), BF16)
    shapes = [(product, BF16)] * QUARTERS
    shapes += [half, half, (user_residuals.shape, BF16), ((block, rows), BF16)]
    arrays = [pltpu.with_memory_space_constraint(v, pltpu.HBM) for v in (basis, atoms, user_residuals)]
    results = call(
        load_kernel,
        shapes,
        atoms.size * count,
        *arrays,
        in_specs=[HBM] * 3,
        scratch=[pltpu.VMEM(atoms.shape, BF16), pltpu.SemaphoreType.DMA((4,))],
    )
    return results[:QUARTERS], *results[QUARTERS:]


def coef_kernel(swapped, places, basis_ref, rem_ref, *out_refs):
    products(swapped, places, rem_ref[...], basis_ref, out_refs)


def coef_call(swapped, places, basis, rem_low):
    block = rem_low.shape[0]
    quarter = basis.shape[1] // QUARTERS
    shapes = [((block, quarter), BF16 if swapped else F32)] * len(places)
    flops = 2 * rem_low.size * quarter * len(places)
    return call(functools.partial(coef_kernel, swapped, places), shapes, flops, basis, rem_low)


def image_kernel(swapped, places, basis_ref, rem_ref, *refs):
    coef_refs, out_refs = refs[: len(places)], refs[len(places) :]
    total = rem_ref[...].astype(F32)
    quarter = basis_ref.shape[1] // QUARTERS
    turn = turns(halves()[swapped])
    for place, coef_ref in zip(places, coef_refs):
        start = pl.multiple_of((turn ^ place) * quarter, quarter)
        columns = basis_ref[:, pl.ds(start, quarter)]
        total = total - lax.dot_general(coef_ref[...], columns, NT, preferred_element_type=F32)
    for out_ref in out_refs:
        out_ref[...] = total.astype(out_ref.dtype)


def image_call(swapped, places, basis, rem, coefs, dtypes):
    shapes = [(rem.shape, dtype) for dtype in dtypes]
    flops = 2 * rem.size * coefs[0].shape[1] * len(places)
    return call(functools.partial(image_kernel, swapped, places), shapes, flops, basis, rem, *coefs)


def sweep(own_half, other_half, rem, own, other, m_total, dtypes):
    got = {place: swap(other[place], CORE) for place in (3, 2, 1, 0)}
    sent = {place: swap((own[place] + got[place]).astype(BF16), place_masks(place)) for place in (3, 2, 1)}
    total = own[0] + got[0] + sent[3] + sent[2] + sent[1]
    for masks in quarter_masks():
        total = total + swap(total.astype(BF16), masks)
    coef = {0: (total / m_total).astype(BF16)}
    for place in (3, 2, 1):
        coef[place] = swap(coef[0], place_masks(place))
    other = {place: swap(coef[place], CORE) for place in (0, 3, 2, 1)}
    (rem,) = image_call(False, (0, 3), own_half, rem, [coef[0], coef[3]], [F32])
    (rem,) = image_call(True, (0, 3), other_half, rem, [other[0], other[3]], [F32])
    (rem,) = image_call(False, (2, 1), own_half, rem, [coef[2], coef[1]], [F32])
    return image_call(True, (2, 1), other_half, rem, [other[2], other[1]], dtypes)


def plain_sweep(basis, rem, rem_low, m_total):
    coef = jnp.einsum("br,rk->bk", rem_low, basis, preferred_element_type=F32)
    coef_low = (lax.psum(coef, "rows") / m_total).astype(BF16)
    image = lax.dot_general(coef_low, basis, NT, preferred_element_type=F32)
    rem = rem - lax.psum(image, "users")
    return rem, rem.astype(BF16)


def small_kernel(turned_ref, user_ref, own_ref, other_ref, rem_ref):
    turned = turned_ref[...]
    rem = turned.T
    gram = jnp.dot(turned, rem, preferred_element_type=F32)
    coupling = jnp.dot(turned, user_ref[...], preferred_element_type=F32)
    first = (lax.axis_index("rows") & 1) == 0
    own_ref[...] = jnp.where(first, gram, coupling)
    other_ref[...] = jnp.where(first, coupling, gram)
    rem_ref[...] = rem


def small_parts(turned_low, user_residuals):
    square = ((user_residuals.shape[1],) * 2, F32)
    return call(small_kernel, [square, square, (user_residuals.shape, BF16)], 0, turned_low, user_residuals)


def small_sums(own, other):
    own = own + swap(other, CORE)
    for group in small_masks():
        own = own + sum(swap(own, masks) for masks in group)
    return own, swap(own, CORE)


def inverse_factor(gram):
    size = gram.shape[0]
    group = 32
    lane = lax.broadcasted_iota(jnp.int32, (8, size), 1)
    row = lax.broadcasted_iota(jnp.int32, (8, size), 0)
    panels = [gram[i : i + 8] for i in range(0, size, 8)]
    result = []

    def across(value, index):
        return jnp.broadcast_to(value[:, index : index + 1], (8, size))

    def down(value, index):
        return jnp.broadcast_to(value[index : index + 1], (8, size))

    for top in range(0, size, group):
        end = min(top + group, size)
        scaled = []
        for first in range(top, end, 8):
            panel = panels[first // 8]
            inside = (lane >= first) & (lane < first + 8)
            columns = [across(panel, first + c) for c in range(8)]
            full = jnp.where(inside, (lane == row + first).astype(F32), panel)
            lower, pivots = full, columns[0]
            for s in range(8):
                pivot, line = down(columns[s], s), down(full, s)
                if s:
                    lower, pivots = jnp.where(row == s, line, lower), jnp.where(row == s, pivot, pivots)
                factor = jnp.where(row == s, 0.0, columns[s] * (1.0 / pivot))
                for c in range(s + 1, 8):
                    columns[c] = columns[c] - factor * down(columns[c], s)
                full = full - factor * line
            full = full * (1.0 / pivots)
            lower = lower * lax.rsqrt(pivots)
            scaled.append(jnp.where((lane > row + first) & (lane < end), 0.0, lower))
            for later in range(first + 8, end, 8):
                value = panels[later // 8]
                total = jnp.where(inside, 0.0, value)
                for c in range(8):
                    total = total - across(value, first + c) * down(full, c)
                panels[later // 8] = total
        result += [jnp.where(lane < end, value, 0.0) for value in scaled]
        if end < size:
            rows = jnp.concatenate(scaled)
            update = jnp.dot(
                rows.T[end:], rows, precision=lax.Precision.HIGHEST, preferred_element_type=F32
            )
            inside = (lane >= top) & (lane < end)
            for first in range(end, size, 8):
                value = jnp.where(inside, 0.0, panels[first // 8])
                panels[first // 8] = value - update[first - end : first - end + 8]
    return jnp.concatenate(result)


def thirds(value):
    high = value.astype(BF16)
    rest = value - high.astype(F32)
    middle = rest.astype(BF16)
    return high, middle, (rest - middle.astype(F32)).astype(BF16)


def finish_kernel(m_total, own_ref, other_ref, rem_ref, user_ref, block_ref, updated_ref):
    first = (lax.axis_index("rows") & 1) == 0
    own, other = own_ref[...], other_ref[...]
    inverse = inverse_factor(jnp.where(first, own, other) * (1.0 / m_total))
    rem = rem_ref[...]
    parts = [lax.dot_general(rem, part, NT, preferred_element_type=F32) for part in thirds(inverse)]
    block = (parts[2] + parts[1] + parts[0]).astype(BF16)
    coupling = jnp.where(first, other, own) * (1.0 / m_total)
    weights = jnp.dot(inverse, coupling, precision=lax.Precision.HIGHEST, preferred_element_type=F32)
    block_ref[...] = block
    image = jnp.dot(block, weights.astype(BF16), preferred_element_type=F32)
    updated_ref[...] = (user_ref[...].astype(F32) - image).astype(BF16)


def finish(own, other, rem_low, user_residuals, m_total):
    shapes = [(v.shape, BF16) for v in (rem_low, user_residuals)]
    return tuple(call(functools.partial(finish_kernel, m_total), shapes, 0, own, other, rem_low, user_residuals))


def plain_finish(remainder_low, gram_total, coupling_total, user_residuals, m_total):
    factor_lower = jnp.linalg.cholesky(gram_total / m_total)
    identity = jnp.eye(factor_lower.shape[0], dtype=F32)
    inverse = jax.scipy.linalg.solve_triangular(factor_lower, identity, lower=True)
    new_block = jnp.dot(remainder_low.astype(F32), inverse.T, precision=lax.Precision.HIGHEST).astype(BF16)
    weights = jnp.dot(inverse, coupling_total / m_total, precision=lax.Precision.HIGHEST).astype(BF16)
    updated = user_residuals.astype(F32) - jnp.dot(new_block, weights, preferred_element_type=F32)
    return (new_block, updated.astype(BF16))


def plain_local(old_basis, new_atoms, user_residuals):
    m_total = float(old_basis.shape[0] * lax.axis_size("rows"))
    rem, rem_low = new_atoms.T.astype(F32), new_atoms.T
    for _ in range(2):
        rem, rem_low = plain_sweep(old_basis, rem, rem_low, m_total)
    gram = lax.dot_general(rem_low, rem_low, NT, preferred_element_type=F32)
    coupling = jnp.dot(rem_low, user_residuals, preferred_element_type=F32)
    gram, coupling = lax.psum((gram, coupling), "rows")
    return plain_finish(rem_low.T, gram, coupling, user_residuals, m_total)


def local(old_basis, new_atoms, user_residuals):
    rows, atoms = old_basis.shape
    block = new_atoms.shape[1]
    size = lax.axis_size("rows")
    users = lax.axis_size("users")
    m_total = float(rows * size)
    power = size >= 32 and size & (size - 1) == 0
    tiled = rows % 128 == 0 and atoms % (2 * QUARTERS * 128) == 0
    if not power or not tiled or block != 128 or user_residuals.shape[1] != block:
        return plain_local(old_basis, new_atoms, user_residuals)

    other, other_half, own_half, user_rows, rem_low = first_products(old_basis, new_atoms, user_residuals)
    rem = rem_low
    for last in (False, True):
        if last:
            last_place = coef_call(True, (3,), other_half, rem_low)
            other = coef_call(True, (0, 1, 2), other_half, rem_low) + last_place
        own = coef_call(False, (0, 1, 2, 3), own_half, rem_low)
        dtypes = [BF16] if last and users == 1 else [F32, BF16]
        start = rem if users == 1 else jnp.zeros(rem.shape, F32)
        *new, rem_low = sweep(own_half, other_half, start, own, other, m_total, dtypes)
        if users == 1:
            rem = new[0] if new else rem
        else:
            rem = rem.astype(F32) + lax.psum(new[0], "users")
            rem_low = rem.astype(BF16)
    own, other, rem_low = small_parts(rem_low, user_rows)
    own, other = small_sums(own, other)
    return finish(own, other, rem_low, user_rows, m_total)


def solution(mesh):
    in_specs = (P("rows", "users"), P("rows", None), P("rows", "users"))
    out_specs = (P("rows", None), P("rows", "users"))
    return jax.shard_map(local, mesh=mesh, in_specs=in_specs, out_specs=out_specs, check_vma=False)
```

```python
import functools

import jax
import jax.numpy as jnp
from jax import lax
from jax.experimental import pallas as pl
from jax.experimental.pallas import tpu as pltpu
from jax.sharding import PartitionSpec as P

BF16, F32 = jnp.bfloat16, jnp.float32
VMEM = pl.BlockSpec(memory_space=pltpu.VMEM)
HBM = pl.BlockSpec(memory_space=pltpu.HBM)
QUARTERS = 4
NT = (((1,), (1,)), ((), ()))


CORE = (1, 1)
SHARE = ((2, 4), (8, 2))


def later_bits(first):
    return [1 << bit for bit in range(first, (lax.axis_size("rows") - 1).bit_length())]


def quarter_masks():
    return [(8, 16), (16, 4)] + [(bit, bit) for bit in later_bits(5)]


def small_masks():
    plane = [place_masks(place) for place in (3, 2, 1)]
    others = [(16, 16), (24, 20), (8, 4)]
    return [plane, others] + [[(bit, bit)] for bit in later_bits(5)]


def place_masks(place):
    return tuple((place >> 1) * high + (place & 1) * low for high, low in SHARE)


def swap(value, masks):
    size = lax.axis_size("rows")
    return lax.ppermute(value, "rows", [(i, i ^ masks[i & 1]) for i in range(size)])


def call(kernel, shapes, flops, *operands, in_specs=None, scratch=()):
    return pl.pallas_call(
        kernel,
        in_specs=in_specs or [VMEM] * len(operands),
        out_specs=[VMEM] * len(shapes),
        out_shape=[jax.ShapeDtypeStruct(*shape) for shape in shapes],
        scratch_shapes=scratch,
        compiler_params=pltpu.CompilerParams(vmem_limit_bytes=32 * 2**20),
        cost_estimate=pl.CostEstimate(flops=flops, bytes_accessed=0, transcendentals=0),
    )(*operands)


def turns(half):
    me = lax.axis_index("rows")
    turn = [2 * jnp.where(me & high, 1, 0) + jnp.where(me & low, 1, 0) for high, low in SHARE]
    return jnp.where(half == 0, turn[0], turn[1])


def halves():
    core = lax.axis_index("rows") & 1
    return core, 1 - core


def products(swapped, places, rem, basis_ref, out_refs):
    quarter = basis_ref.shape[1] // QUARTERS
    turn = turns(halves()[swapped])
    for place, out_ref in zip(places, out_refs):
        start = pl.multiple_of((turn ^ place) * quarter, quarter)
        product = jnp.dot(rem, basis_ref[:, pl.ds(start, quarter)], preferred_element_type=F32)
        out_ref[...] = product.astype(out_ref.dtype)


def load_kernel(basis_ref, atoms_ref, user_ref, *refs):
    other_refs, refs = refs[:QUARTERS], refs[QUARTERS:]
    other_half_ref, own_half_ref, user_rows_ref, turned_ref, rows_ref, sems = refs
    own, other = halves()

    def half_copy(half, half_ref, sem):
        columns = half_ref.shape[1]
        start = pl.multiple_of(half * columns, columns)
        return pltpu.make_async_copy(basis_ref.at[:, pl.ds(start, columns)], half_ref, sem)

    copies = [
        pltpu.make_async_copy(atoms_ref, rows_ref, sems.at[0]),
        half_copy(other, other_half_ref, sems.at[1]),
        half_copy(own, own_half_ref, sems.at[2]),
        pltpu.make_async_copy(user_ref, user_rows_ref, sems.at[3]),
    ]
    for copy in copies:
        copy.start()
    copies[0].wait()
    rem = rows_ref[...].T
    turned_ref[...] = rem
    copies[1].wait()
    products(1, range(QUARTERS), rem, other_half_ref, other_refs)
    for copy in copies[2:]:
        copy.wait()


def first_products(basis, atoms, user_residuals):
    rows, count = basis.shape
    block = atoms.shape[1]
    product = (block, count // (2 * QUARTERS))
    half = ((rows, count // 2), BF16)
    shapes = [(product, BF16)] * QUARTERS
    shapes += [half, half, (user_residuals.shape, BF16), ((block, rows), BF16)]
    arrays = [pltpu.with_memory_space_constraint(v, pltpu.HBM) for v in (basis, atoms, user_residuals)]
    results = call(
        load_kernel,
        shapes,
        atoms.size * count,
        *arrays,
        in_specs=[HBM] * 3,
        scratch=[pltpu.VMEM(atoms.shape, BF16), pltpu.SemaphoreType.DMA((4,))],
    )
    return results[:QUARTERS], *results[QUARTERS:]


def coef_kernel(swapped, places, basis_ref, rem_ref, *out_refs):
    products(swapped, places, rem_ref[...], basis_ref, out_refs)


def coef_call(swapped, places, basis, rem_low):
    block = rem_low.shape[0]
    quarter = basis.shape[1] // QUARTERS
    shapes = [((block, quarter), BF16 if swapped else F32)] * len(places)
    flops = 2 * rem_low.size * quarter * len(places)
    return call(functools.partial(coef_kernel, swapped, places), shapes, flops, basis, rem_low)


def image_kernel(swapped, places, basis_ref, rem_ref, *refs):
    coef_refs, out_refs = refs[: len(places)], refs[len(places) :]
    total = rem_ref[...].astype(F32)
    quarter = basis_ref.shape[1] // QUARTERS
    turn = turns(halves()[swapped])
    for place, coef_ref in zip(places, coef_refs):
        start = pl.multiple_of((turn ^ place) * quarter, quarter)
        columns = basis_ref[:, pl.ds(start, quarter)]
        total = total - lax.dot_general(coef_ref[...], columns, NT, preferred_element_type=F32)
    for out_ref in out_refs:
        out_ref[...] = total.astype(out_ref.dtype)


def image_call(swapped, places, basis, rem, coefs, dtypes):
    shapes = [(rem.shape, dtype) for dtype in dtypes]
    flops = 2 * rem.size * coefs[0].shape[1] * len(places)
    return call(functools.partial(image_kernel, swapped, places), shapes, flops, basis, rem, *coefs)


def sweep(own_half, other_half, rem, own, other, m_total, dtypes):
    got = {place: swap(other[place], CORE) for place in (3, 2, 1, 0)}
    sent = {place: swap((own[place] + got[place]).astype(BF16), place_masks(place)) for place in (3, 2, 1)}
    total = own[0] + got[0] + sent[3] + sent[2] + sent[1]
    for masks in quarter_masks():
        total = total + swap(total.astype(BF16), masks)
    coef = {0: (total / m_total).astype(BF16)}
    for place in (3, 2, 1):
        coef[place] = swap(coef[0], place_masks(place))
    other = {place: swap(coef[place], CORE) for place in (0, 3, 2, 1)}
    (rem,) = image_call(False, (0, 3), own_half, rem, [coef[0], coef[3]], [F32])
    (rem,) = image_call(True, (0, 3), other_half, rem, [other[0], other[3]], [F32])
    (rem,) = image_call(False, (2, 1), own_half, rem, [coef[2], coef[1]], [F32])
    return image_call(True, (2, 1), other_half, rem, [other[2], other[1]], dtypes)


def plain_sweep(basis, rem, rem_low, m_total):
    coef = jnp.einsum("br,rk->bk", rem_low, basis, preferred_element_type=F32)
    coef_low = (lax.psum(coef, "rows") / m_total).astype(BF16)
    image = lax.dot_general(coef_low, basis, NT, preferred_element_type=F32)
    rem = rem - lax.psum(image, "users")
    return rem, rem.astype(BF16)


def small_kernel(turned_ref, user_ref, own_ref, other_ref, rem_ref):
    turned = turned_ref[...]
    rem = turned.T
    gram = jnp.dot(turned, rem, preferred_element_type=F32)
    coupling = jnp.dot(turned, user_ref[...], preferred_element_type=F32)
    first = (lax.axis_index("rows") & 1) == 0
    own_ref[...] = jnp.where(first, gram, coupling)
    other_ref[...] = jnp.where(first, coupling, gram)
    rem_ref[...] = rem


def small_parts(turned_low, user_residuals):
    square = ((user_residuals.shape[1],) * 2, F32)
    return call(small_kernel, [square, square, (user_residuals.shape, BF16)], 0, turned_low, user_residuals)


def small_sums(own, other):
    own = own + swap(other, CORE)
    for group in small_masks():
        own = own + sum(swap(own, masks) for masks in group)
    return own, swap(own, CORE)


def inverse_factor(gram):
    size = gram.shape[0]
    group = 32
    lane = lax.broadcasted_iota(jnp.int32, (8, size), 1)
    row = lax.broadcasted_iota(jnp.int32, (8, size), 0)
    panels = [gram[i : i + 8] for i in range(0, size, 8)]
    result = []

    def across(value, index):
        return jnp.broadcast_to(value[:, index : index + 1], (8, size))

    def down(value, index):
        return jnp.broadcast_to(value[index : index + 1], (8, size))

    for top in range(0, size, group):
        end = min(top + group, size)
        scaled = []
        for first in range(top, end, 8):
            panel = panels[first // 8]
            inside = (lane >= first) & (lane < first + 8)
            columns = [across(panel, first + c) for c in range(8)]
            full = jnp.where(inside, (lane == row + first).astype(F32), panel)
            lower, pivots = full, columns[0]
            for s in range(8):
                pivot, line = down(columns[s], s), down(full, s)
                if s:
                    lower, pivots = jnp.where(row == s, line, lower), jnp.where(row == s, pivot, pivots)
                factor = jnp.where(row == s, 0.0, columns[s] * (1.0 / pivot))
                for c in range(s + 1, 8):
                    columns[c] = columns[c] - factor * down(columns[c], s)
                full = full - factor * line
            full = full * (1.0 / pivots)
            lower = lower * lax.rsqrt(pivots)
            scaled.append(jnp.where((lane > row + first) & (lane < end), 0.0, lower))
            for later in range(first + 8, end, 8):
                value = panels[later // 8]
                total = jnp.where(inside, 0.0, value)
                for c in range(8):
                    total = total - across(value, first + c) * down(full, c)
                panels[later // 8] = total
        result += [jnp.where(lane < end, value, 0.0) for value in scaled]
        if end < size:
            rows = jnp.concatenate(scaled)
            update = jnp.dot(
                rows.T[end:], rows, precision=lax.Precision.HIGHEST, preferred_element_type=F32
            )
            inside = (lane >= top) & (lane < end)
            for first in range(end, size, 8):
                value = jnp.where(inside, 0.0, panels[first // 8])
                panels[first // 8] = value - update[first - end : first - end + 8]
    return jnp.concatenate(result)


def thirds(value):
    high = value.astype(BF16)
    rest = value - high.astype(F32)
    middle = rest.astype(BF16)
    return high, middle, (rest - middle.astype(F32)).astype(BF16)


def finish_kernel(m_total, own_ref, other_ref, rem_ref, user_ref, block_ref, updated_ref):
    first = (lax.axis_index("rows") & 1) == 0
    own, other = own_ref[...], other_ref[...]
    inverse = inverse_factor(jnp.where(first, own, other) * (1.0 / m_total))
    rem = rem_ref[...]
    parts = [lax.dot_general(rem, part, NT, preferred_element_type=F32) for part in thirds(inverse)]
    block = (parts[2] + parts[1] + parts[0]).astype(BF16)
    coupling = jnp.where(first, other, own) * (1.0 / m_total)
    weights = jnp.dot(inverse, coupling, precision=lax.Precision.HIGHEST, preferred_element_type=F32)
    block_ref[...] = block
    image = jnp.dot(block, weights.astype(BF16), preferred_element_type=F32)
    updated_ref[...] = (user_ref[...].astype(F32) - image).astype(BF16)


def finish(own, other, rem_low, user_residuals, m_total):
    shapes = [(v.shape, BF16) for v in (rem_low, user_residuals)]
    return tuple(call(functools.partial(finish_kernel, m_total), shapes, 0, own, other, rem_low, user_residuals))


def plain_finish(remainder_low, gram_total, coupling_total, user_residuals, m_total):
    factor_lower = jnp.linalg.cholesky(gram_total / m_total)
    identity = jnp.eye(factor_lower.shape[0], dtype=F32)
    inverse = jax.scipy.linalg.solve_triangular(factor_lower, identity, lower=True)
    new_block = jnp.dot(remainder_low.astype(F32), inverse.T, precision=lax.Precision.HIGHEST).astype(BF16)
    weights = jnp.dot(inverse, coupling_total / m_total, precision=lax.Precision.HIGHEST).astype(BF16)
    updated = user_residuals.astype(F32) - jnp.dot(new_block, weights, preferred_element_type=F32)
    return (new_block, updated.astype(BF16))


def plain_local(old_basis, new_atoms, user_residuals):
    m_total = float(old_basis.shape[0] * lax.axis_size("rows"))
    rem, rem_low = new_atoms.T.astype(F32), new_atoms.T
    for _ in range(2):
        rem, rem_low = plain_sweep(old_basis, rem, rem_low, m_total)
    gram = lax.dot_general(rem_low, rem_low, NT, preferred_element_type=F32)
    coupling = jnp.dot(rem_low, user_residuals, preferred_element_type=F32)
    gram, coupling = lax.psum((gram, coupling), "rows")
    return plain_finish(rem_low.T, gram, coupling, user_residuals, m_total)


def local(old_basis, new_atoms, user_residuals):
    rows, atoms = old_basis.shape
    block = new_atoms.shape[1]
    size = lax.axis_size("rows")
    users = lax.axis_size("users")
    m_total = float(rows * size)
    power = size >= 32 and size & (size - 1) == 0
    tiled = rows % 128 == 0 and atoms % (2 * QUARTERS * 128) == 0
    if not power or not tiled or block != 128 or user_residuals.shape[1] != block:
        return plain_local(old_basis, new_atoms, user_residuals)

    other, other_half, own_half, user_rows, rem_low = first_products(old_basis, new_atoms, user_residuals)
    rem = rem_low
    for last in (False, True):
        if last:
            last_place = coef_call(True, (3,), other_half, rem_low)
            other = coef_call(True, (0, 1, 2), other_half, rem_low) + last_place
        own = coef_call(False, (0, 1, 2, 3), own_half, rem_low)
        dtypes = [BF16] if last and users == 1 else [F32, BF16]
        start = rem if users == 1 else jnp.zeros(rem.shape, F32)
        *new, rem_low = sweep(own_half, other_half, start, own, other, m_total, dtypes)
        if users == 1:
            rem = new[0] if new else rem
        else:
            rem = rem.astype(F32) + lax.psum(new[0], "users")
            rem_low = rem.astype(BF16)
    own, other, rem_low = small_parts(rem_low, user_rows)
    own, other = small_sums(own, other)
    return finish(own, other, rem_low, user_rows, m_total)


def solution(mesh):
    in_specs = (P("rows", "users"), P("rows", None), P("rows", "users"))
    out_specs = (P("rows", None), P("rows", "users"))
    return jax.shard_map(local, mesh=mesh, in_specs=in_specs, out_specs=out_specs, check_vma=False)
```

```python
import functools

import jax
import jax.numpy as jnp
from jax import lax
from jax.experimental import pallas as pl
from jax.experimental.pallas import tpu as pltpu
from jax.sharding import PartitionSpec as P

BF16, F32 = jnp.bfloat16, jnp.float32
VMEM = pl.BlockSpec(memory_space=pltpu.VMEM)
HBM = pl.BlockSpec(memory_space=pltpu.HBM)
QUARTERS = 4
NT = (((1,), (1,)), ((), ()))


CORE = (1, 1)
SHARE = ((2, 4), (8, 2))


def later_bits(first):
    return [1 << bit for bit in range(first, (lax.axis_size("rows") - 1).bit_length())]


def quarter_masks():
    return [(8, 16), (16, 4)] + [(bit, bit) for bit in later_bits(5)]


def small_masks():
    plane = [place_masks(place) for place in (3, 2, 1)]
    others = [(16, 16), (24, 20), (8, 4)]
    return [plane, others] + [[(bit, bit)] for bit in later_bits(5)]


def place_masks(place):
    return tuple((place >> 1) * high + (place & 1) * low for high, low in SHARE)


def swap(value, masks):
    size = lax.axis_size("rows")
    return lax.ppermute(value, "rows", [(i, i ^ masks[i & 1]) for i in range(size)])


def call(kernel, shapes, flops, *operands, in_specs=None, scratch=()):
    return pl.pallas_call(
        kernel,
        in_specs=in_specs or [VMEM] * len(operands),
        out_specs=[VMEM] * len(shapes),
        out_shape=[jax.ShapeDtypeStruct(*shape) for shape in shapes],
        scratch_shapes=scratch,
        compiler_params=pltpu.CompilerParams(vmem_limit_bytes=32 * 2**20),
        cost_estimate=pl.CostEstimate(flops=flops, bytes_accessed=0, transcendentals=0),
    )(*operands)


def turns(half):
    me = lax.axis_index("rows")
    turn = [2 * jnp.where(me & high, 1, 0) + jnp.where(me & low, 1, 0) for high, low in SHARE]
    return jnp.where(half == 0, turn[0], turn[1])


def halves():
    core = lax.axis_index("rows") & 1
    return core, 1 - core


def products(swapped, places, rem, basis_ref, out_refs):
    quarter = basis_ref.shape[1] // QUARTERS
    turn = turns(halves()[swapped])
    for place, out_ref in zip(places, out_refs):
        start = pl.multiple_of((turn ^ place) * quarter, quarter)
        product = jnp.dot(rem, basis_ref[:, pl.ds(start, quarter)], preferred_element_type=F32)
        out_ref[...] = product.astype(out_ref.dtype)


def load_kernel(basis_ref, atoms_ref, user_ref, *refs):
    other_refs, refs = refs[:QUARTERS], refs[QUARTERS:]
    other_half_ref, own_half_ref, user_rows_ref, turned_ref, rows_ref, sems = refs
    own, other = halves()

    def half_copy(half, half_ref, sem):
        columns = half_ref.shape[1]
        start = pl.multiple_of(half * columns, columns)
        return pltpu.make_async_copy(basis_ref.at[:, pl.ds(start, columns)], half_ref, sem)

    copies = [
        pltpu.make_async_copy(atoms_ref, rows_ref, sems.at[0]),
        half_copy(other, other_half_ref, sems.at[1]),
        half_copy(own, own_half_ref, sems.at[2]),
        pltpu.make_async_copy(user_ref, user_rows_ref, sems.at[3]),
    ]
    for copy in copies:
        copy.start()
    copies[0].wait()
    rem = rows_ref[...].T
    turned_ref[...] = rem
    copies[1].wait()
    products(1, range(QUARTERS), rem, other_half_ref, other_refs)
    for copy in copies[2:]:
        copy.wait()


def first_products(basis, atoms, user_residuals):
    rows, count = basis.shape
    block = atoms.shape[1]
    product = (block, count // (2 * QUARTERS))
    half = ((rows, count // 2), BF16)
    shapes = [(product, BF16)] * QUARTERS
    shapes += [half, half, (user_residuals.shape, BF16), ((block, rows), BF16)]
    arrays = [pltpu.with_memory_space_constraint(v, pltpu.HBM) for v in (basis, atoms, user_residuals)]
    results = call(
        load_kernel,
        shapes,
        atoms.size * count,
        *arrays,
        in_specs=[HBM] * 3,
        scratch=[pltpu.VMEM(atoms.shape, BF16), pltpu.SemaphoreType.DMA((4,))],
    )
    return results[:QUARTERS], *results[QUARTERS:]


def coef_kernel(swapped, places, basis_ref, rem_ref, *out_refs):
    products(swapped, places, rem_ref[...], basis_ref, out_refs)


def coef_call(swapped, places, basis, rem_low):
    block = rem_low.shape[0]
    quarter = basis.shape[1] // QUARTERS
    shapes = [((block, quarter), BF16 if swapped else F32)] * len(places)
    flops = 2 * rem_low.size * quarter * len(places)
    return call(functools.partial(coef_kernel, swapped, places), shapes, flops, basis, rem_low)


def image_kernel(swapped, places, basis_ref, rem_ref, *refs):
    coef_refs, out_refs = refs[: len(places)], refs[len(places) :]
    total = rem_ref[...].astype(F32)
    quarter = basis_ref.shape[1] // QUARTERS
    turn = turns(halves()[swapped])
    for place, coef_ref in zip(places, coef_refs):
        start = pl.multiple_of((turn ^ place) * quarter, quarter)
        columns = basis_ref[:, pl.ds(start, quarter)]
        total = total - lax.dot_general(coef_ref[...], columns, NT, preferred_element_type=F32)
    for out_ref in out_refs:
        out_ref[...] = total.astype(out_ref.dtype)


def image_call(swapped, places, basis, rem, coefs, dtypes):
    shapes = [(rem.shape, dtype) for dtype in dtypes]
    flops = 2 * rem.size * coefs[0].shape[1] * len(places)
    return call(functools.partial(image_kernel, swapped, places), shapes, flops, basis, rem, *coefs)


def sweep(own_half, other_half, rem, own, other, m_total, dtypes):
    got = {place: swap(other[place], CORE) for place in (3, 2, 1, 0)}
    sent = {place: swap((own[place] + got[place]).astype(BF16), place_masks(place)) for place in (3, 2, 1)}
    total = own[0] + got[0] + sent[3] + sent[2] + sent[1]
    for masks in quarter_masks():
        total = total + swap(total.astype(BF16), masks)
    coef = {0: (total / m_total).astype(BF16)}
    for place in (3, 2, 1):
        coef[place] = swap(coef[0], place_masks(place))
    other = {place: swap(coef[place], CORE) for place in (0, 3, 2, 1)}
    (rem,) = image_call(True, (0, 3), other_half, rem, [other[0], other[3]], [F32])
    (rem,) = image_call(False, (0, 3, 2, 1), own_half, rem, [coef[0], coef[3], coef[2], coef[1]], [F32])
    return image_call(True, (2, 1), other_half, rem, [other[2], other[1]], dtypes)


def plain_sweep(basis, rem, rem_low, m_total):
    coef = jnp.einsum("br,rk->bk", rem_low, basis, preferred_element_type=F32)
    coef_low = (lax.psum(coef, "rows") / m_total).astype(BF16)
    image = lax.dot_general(coef_low, basis, NT, preferred_element_type=F32)
    rem = rem - lax.psum(image, "users")
    return rem, rem.astype(BF16)


def small_kernel(turned_ref, user_ref, own_ref, other_ref, rem_ref):
    turned = turned_ref[...]
    rem = turned.T
    gram = jnp.dot(turned, rem, preferred_element_type=F32)
    coupling = jnp.dot(turned, user_ref[...], preferred_element_type=F32)
    first = (lax.axis_index("rows") & 1) == 0
    own_ref[...] = jnp.where(first, gram, coupling)
    other_ref[...] = jnp.where(first, coupling, gram)
    rem_ref[...] = rem


def small_parts(turned_low, user_residuals):
    square = ((user_residuals.shape[1],) * 2, F32)
    return call(small_kernel, [square, square, (user_residuals.shape, BF16)], 0, turned_low, user_residuals)


def small_sums(own, other):
    own = own + swap(other, CORE)
    for group in small_masks():
        own = own + sum(swap(own, masks) for masks in group)
    return own, swap(own, CORE)


def inverse_factor(gram):
    size = gram.shape[0]
    group = 32
    lane = lax.broadcasted_iota(jnp.int32, (8, size), 1)
    row = lax.broadcasted_iota(jnp.int32, (8, size), 0)
    panels = [gram[i : i + 8] for i in range(0, size, 8)]
    result = []

    def across(value, index):
        return jnp.broadcast_to(value[:, index : index + 1], (8, size))

    def down(value, index):
        return jnp.broadcast_to(value[index : index + 1], (8, size))

    for top in range(0, size, group):
        end = min(top + group, size)
        scaled = []
        for first in range(top, end, 8):
            panel = panels[first // 8]
            inside = (lane >= first) & (lane < first + 8)
            columns = [across(panel, first + c) for c in range(8)]
            full = jnp.where(inside, (lane == row + first).astype(F32), panel)
            lower, pivots = full, columns[0]
            for s in range(8):
                pivot, line = down(columns[s], s), down(full, s)
                if s:
                    lower, pivots = jnp.where(row == s, line, lower), jnp.where(row == s, pivot, pivots)
                factor = jnp.where(row == s, 0.0, columns[s] * (1.0 / pivot))
                for c in range(s + 1, 8):
                    columns[c] = columns[c] - factor * down(columns[c], s)
                full = full - factor * line
            full = full * (1.0 / pivots)
            lower = lower * lax.rsqrt(pivots)
            scaled.append(jnp.where((lane > row + first) & (lane < end), 0.0, lower))
            for later in range(first + 8, end, 8):
                value = panels[later // 8]
                total = jnp.where(inside, 0.0, value)
                for c in range(8):
                    total = total - across(value, first + c) * down(full, c)
                panels[later // 8] = total
        result += [jnp.where(lane < end, value, 0.0) for value in scaled]
        if end < size:
            rows = jnp.concatenate(scaled)
            update = jnp.dot(
                rows.T[end:], rows, precision=lax.Precision.HIGHEST, preferred_element_type=F32
            )
            inside = (lane >= top) & (lane < end)
            for first in range(end, size, 8):
                value = jnp.where(inside, 0.0, panels[first // 8])
                panels[first // 8] = value - update[first - end : first - end + 8]
    return jnp.concatenate(result)


def thirds(value):
    high = value.astype(BF16)
    rest = value - high.astype(F32)
    middle = rest.astype(BF16)
    return high, middle, (rest - middle.astype(F32)).astype(BF16)


def finish_kernel(m_total, own_ref, other_ref, rem_ref, user_ref, block_ref, updated_ref):
    first = (lax.axis_index("rows") & 1) == 0
    own, other = own_ref[...], other_ref[...]
    inverse = inverse_factor(jnp.where(first, own, other) * (1.0 / m_total))
    rem = rem_ref[...]
    parts = [lax.dot_general(rem, part, NT, preferred_element_type=F32) for part in thirds(inverse)]
    block = (parts[2] + parts[1] + parts[0]).astype(BF16)
    coupling = jnp.where(first, other, own) * (1.0 / m_total)
    weights = jnp.dot(inverse, coupling, precision=lax.Precision.HIGHEST, preferred_element_type=F32)
    block_ref[...] = block
    image = jnp.dot(block, weights.astype(BF16), preferred_element_type=F32)
    updated_ref[...] = (user_ref[...].astype(F32) - image).astype(BF16)


def finish(own, other, rem_low, user_residuals, m_total):
    shapes = [(v.shape, BF16) for v in (rem_low, user_residuals)]
    return tuple(call(functools.partial(finish_kernel, m_total), shapes, 0, own, other, rem_low, user_residuals))


def plain_finish(remainder_low, gram_total, coupling_total, user_residuals, m_total):
    factor_lower = jnp.linalg.cholesky(gram_total / m_total)
    identity = jnp.eye(factor_lower.shape[0], dtype=F32)
    inverse = jax.scipy.linalg.solve_triangular(factor_lower, identity, lower=True)
    new_block = jnp.dot(remainder_low.astype(F32), inverse.T, precision=lax.Precision.HIGHEST).astype(BF16)
    weights = jnp.dot(inverse, coupling_total / m_total, precision=lax.Precision.HIGHEST).astype(BF16)
    updated = user_residuals.astype(F32) - jnp.dot(new_block, weights, preferred_element_type=F32)
    return (new_block, updated.astype(BF16))


def plain_local(old_basis, new_atoms, user_residuals):
    m_total = float(old_basis.shape[0] * lax.axis_size("rows"))
    rem, rem_low = new_atoms.T.astype(F32), new_atoms.T
    for _ in range(2):
        rem, rem_low = plain_sweep(old_basis, rem, rem_low, m_total)
    gram = lax.dot_general(rem_low, rem_low, NT, preferred_element_type=F32)
    coupling = jnp.dot(rem_low, user_residuals, preferred_element_type=F32)
    gram, coupling = lax.psum((gram, coupling), "rows")
    return plain_finish(rem_low.T, gram, coupling, user_residuals, m_total)


def local(old_basis, new_atoms, user_residuals):
    rows, atoms = old_basis.shape
    block = new_atoms.shape[1]
    size = lax.axis_size("rows")
    users = lax.axis_size("users")
    m_total = float(rows * size)
    power = size >= 32 and size & (size - 1) == 0
    tiled = rows % 128 == 0 and atoms % (2 * QUARTERS * 128) == 0
    if not power or not tiled or block != 128 or user_residuals.shape[1] != block:
        return plain_local(old_basis, new_atoms, user_residuals)

    other, other_half, own_half, user_rows, rem_low = first_products(old_basis, new_atoms, user_residuals)
    rem = rem_low
    for last in (False, True):
        if last:
            last_place = coef_call(True, (3,), other_half, rem_low)
            other = coef_call(True, (0, 1, 2), other_half, rem_low) + last_place
        own = coef_call(False, (0, 1, 2, 3), own_half, rem_low)
        dtypes = [BF16] if last and users == 1 else [F32, BF16]
        start = rem if users == 1 else jnp.zeros(rem.shape, F32)
        *new, rem_low = sweep(own_half, other_half, start, own, other, m_total, dtypes)
        if users == 1:
            rem = new[0] if new else rem
        else:
            rem = rem.astype(F32) + lax.psum(new[0], "users")
            rem_low = rem.astype(BF16)
    own, other, rem_low = small_parts(rem_low, user_rows)
    own, other = small_sums(own, other)
    return finish(own, other, rem_low, user_rows, m_total)


def solution(mesh):
    in_specs = (P("rows", "users"), P("rows", None), P("rows", "users"))
    out_specs = (P("rows", None), P("rows", "users"))
    return jax.shard_map(local, mesh=mesh, in_specs=in_specs, out_specs=out_specs, check_vma=False)
```
